512 devices in a mesh: gx: 8 (over y), gy: 8 (over x, core), gz: 8 (over z).
Axes of the slice: x: 4, y: 8, z: 8, core: 2. Of those that a mesh axis runs over, the one named last changes fastest.
Arguments:
- offsets: float32 [3, 16, 16, 16, 128], P(None, 'gx', 'gy', 'gz'), may hold values from -0.5 to 0.5
- lines: float32 [3, 16, 16, 16, 128], P(None, 'gx', 'gy', 'gz'), may hold values from -4 to 4
- burgers: float32 [3, 16, 16, 16, 128], P(None, 'gx', 'gy', 'gz'), may hold values from -4 to 4
- counts: int32 [16, 16, 16], P('gx', 'gy', 'gz'), may hold values from 64 to 128, as said below
- mobility: float32 [16, 16, 16], P('gx', 'gy', 'gz'), may hold values from 0.5 to 2
- stress: float32 [3, 3], replicated, may hold values from -3 to 3
- translation: float32 [128, 128], replicated, may hold values from -0.625 to 0.625
Outputs:
- velocity: float32 [3, 16, 16, 16, 128], P(None, 'gx', 'gy', 'gz')
The draws below stay inside these ranges and needn't reach their ends.
Inputs may be any that keep to these rules, and one draw needn't show every extreme that they name: `counts`: some cell holds 128 live segments.
All inputs are finite; a program needn't handle non-finite values.
Results may differ from the reference program's by a relative error of at most 0.0003.
Values sent between devices are 32-bit elements; how exact they have to be, the bound alone decides.
A program may use at most 64 MiB of HBM per device.

```python
import math
import jax
import jax.numpy as jnp
from jax import lax

SLOTS = 128
TERMS = 35
EXPANSION = 128
NCX = 16
NCY = 16
NCZ = 16
CELLS = 4096


def draw_counts(key, part):
    key = jax.random.fold_in(key, 7)
    primary_key, secondary_key = jax.random.split(key)
    shape = (NCX, NCY, NCZ)
    primary = jax.random.randint(primary_key, shape, 0, SLOTS)
    secondary = jax.random.randint(secondary_key, shape, 0, SLOTS)
    result = SLOTS // 2 + primary * secondary // (2 * SLOTS)
    return result.at[0, 0, 0].set(SLOTS).astype(jnp.int32)


def block_scale(own_key, shape, cuts, low, top_value):
    factor_of = 1.0
    for position, shards_of in cuts:
        heights = jax.random.uniform(jax.random.fold_in(jax.random.fold_in(own_key, 6), position), (shards_of,), jnp.float32, low / len(cuts), top_value / len(cuts))
        factor_of = factor_of * jnp.repeat(jnp.exp(heights), shape[position] // shards_of).reshape((-1,) + (1,) * (len(shape) - 1 - position))
    return factor_of


def scatter_about(own_key, dims, spread, limit, shards=(), kind=jnp.bfloat16):
    entries = spread * jax.random.normal(own_key, dims, jnp.float32)
    if shards:
        entries = entries * block_scale(own_key, dims, shards, -0.22, 0.18)
    return jnp.clip(entries, -limit, limit).astype(kind)


def setup_inputs(seed: int = 0) -> dict:
    key_list = jax.random.split(jax.random.key(seed), 8)
    return {
        "offsets": jnp.clip(jax.random.uniform(key_list[0], (3, NCX, NCY, NCZ, SLOTS), jnp.float32, -0.5, 0.5) * block_scale(key_list[0], (3, NCX, NCY, NCZ, SLOTS), ((1, 8), (2, 8), (3, 8)), -0.4, 0.0), -0.5, 0.5),
        "lines": scatter_about(key_list[1], (3, NCX, NCY, NCZ, SLOTS), 1.0, 4.0, ((1, 8), (2, 8), (3, 8)), jnp.float32),
        "burgers": scatter_about(key_list[2], (3, NCX, NCY, NCZ, SLOTS), 1.0, 4.0, ((1, 8), (2, 8), (3, 8)), jnp.float32),
        "counts": draw_counts(jax.random.fold_in(key_list[7], 71), 0),
        "mobility": jnp.clip(jnp.exp(math.log(2.0) - 1.3862944 * jax.random.uniform(key_list[4], (NCX, NCY, NCZ), jnp.float32) ** block_scale(key_list[4], (NCX, NCY, NCZ), ((0, 8), (1, 8), (2, 8)), -0.2, 0.2)), 0.5, 2.0),
        "stress": scatter_about(key_list[5], (3, 3), 0.5, 3.0, (), jnp.float32),
        "translation": scatter_about(key_list[6], (EXPANSION, EXPANSION), (3 * TERMS) ** -0.5, 0.625, (), jnp.float32),
    }


core_square = 0.0625
near_scale = 0.01
highest = lax.Precision.HIGHEST

def exponent_list():
    result = []
    for first in range(5):
        for second in range(5 - first):
            for third in range(5 - first - second):
                result.append((first, second, third))
    return result

def monomials(relative):
    powers = []
    for column in range(3):
        base = relative[column]
        square = base * base
        powers.append([jnp.ones_like(base), base, square, square * base, square * square])
    return jnp.stack([powers[0][first] * powers[1][second] * powers[2][third] for first, second, third in exponent_list()])

def crossed(left, right):
    return jnp.stack([left[1] * right[2] - left[2] * right[1], left[2] * right[0] - left[0] * right[2], left[0] * right[1] - left[1] * right[0]])

def pair_forces(target, source, shift):
    separation = [shift[column] + source[column][..., None, :] - target[column][..., :, None] for column in range(3)]
    radius_sq = separation[0] * separation[0] + separation[1] * separation[1] + separation[2] * separation[2] + core_square
    inverse = 1.0 / (radius_sq * jnp.sqrt(radius_sq))
    burgers_dot = sum((target[6 + column][..., :, None] * source[6 + column][..., None, :] for column in range(3)))
    line_dot = sum((target[3 + column][..., :, None] * source[3 + column][..., None, :] for column in range(3)))
    target_proj = sum((target[6 + column][..., :, None] * separation[column] for column in range(3)))
    source_proj = sum((source[6 + column][..., None, :] * separation[column] for column in range(3)))
    first_coef = inverse * burgers_dot * line_dot
    second_coef = inverse * target_proj * source_proj / radius_sq
    return jnp.stack([lax.optimization_barrier(jnp.sum(first_coef * separation[column] + second_coef * source[3 + column][..., None, :], -1)) for column in range(3)])

def near_total(inner, padded):
    extent = inner.shape[1:4]
    total = jnp.zeros((3,) + inner.shape[1:], jnp.float32)
    for step_x in (-1, 0, 1):
        for step_y in (-1, 0, 1):
            for step_z in (-1, 0, 1):
                source = padded[:, 1 + step_x:1 + step_x + extent[0], 1 + step_y:1 + step_y + extent[1], 1 + step_z:1 + step_z + extent[2]]
                total = total + pair_forces(inner, source, (float(step_x), float(step_y), float(step_z)))
    return near_scale * total

def cell_moments(poly, charge, slots, width):
    moments = jnp.einsum('kxyzs,cxyzs->xyzck', poly, charge, precision=highest) / slots
    flat = moments.reshape(-1, 3 * poly.shape[0])
    return jnp.pad(flat, ((0, 0), (0, width - flat.shape[1])))

def far_weights(rows_first, rows_second, extents):
    total_sq = jnp.zeros((rows_first[0].shape[0], rows_second[0].shape[0]), jnp.float32)
    largest = jnp.zeros((rows_first[0].shape[0], rows_second[0].shape[0]), jnp.int32)
    for column in range(3):
        spacing = jnp.abs(rows_first[column][:, None] - rows_second[column][None, :]) % extents[column]
        spacing = jnp.minimum(spacing, extents[column] - spacing)
        largest = jnp.maximum(largest, spacing)
        total_sq = total_sq + spacing.astype(jnp.float32) * spacing.astype(jnp.float32)
    return jnp.where(largest > 1, 1.0 / jnp.sqrt(jnp.maximum(total_sq, 1.0)), 0.0).astype(jnp.float32)

def finish(lines, charge, mask, poly, near, coefficients, mobility, stress):
    terms = poly.shape[0]
    blocks = coefficients[..., :3 * terms].reshape(coefficients.shape[:3] + (3, terms))
    far = jnp.einsum('kxyzs,xyzak->axyzs', poly, blocks, precision=highest)
    stressed = jnp.stack([sum((stress[row, column] * charge[column] for column in range(3))) for row in range(3)])
    applied = crossed(stressed, lines)
    force = near + far * mask + applied
    along = lax.optimization_barrier(jnp.sum(force * lines, 0)) / jnp.maximum(lax.optimization_barrier(jnp.sum(lines * lines, 0)), 1.0)
    return mobility[..., None] * mask * (force - along * lines)

def reference(offsets, lines, burgers, counts, mobility, stress, translation):
    slots = offsets.shape[-1]
    mask = (lax.broadcasted_iota(jnp.int32, counts.shape + (slots,), 3) < counts[..., None]).astype(jnp.float32)
    charge = burgers * mask
    stacked = jnp.concatenate([offsets, lines, charge], 0)
    padded = jnp.pad(stacked, ((0, 0), (1, 1), (1, 1), (1, 1), (0, 0)), mode='wrap')

    def slab_force(index):
        slab = lax.dynamic_slice_in_dim(padded, index, 3, 1)
        return near_total(slab[:, 1:2, 1:-1, 1:-1], slab)
    near = lax.map(slab_force, jnp.arange(NCX, dtype=jnp.int32))
    near = jnp.moveaxis(near[:, :, 0], 0, 1)
    poly = monomials(offsets)
    moments = cell_moments(poly, crossed(charge, lines), slots, translation.shape[0])
    cell_index = jnp.arange(CELLS, dtype=jnp.int32)
    columns = (cell_index // (NCY * NCZ), cell_index // NCZ % NCY, cell_index % NCZ)
    block = math.gcd(CELLS, 512)

    def expand(start):
        rows = start + jnp.arange(block, dtype=jnp.int32)
        weights = far_weights((rows // (NCY * NCZ), rows // NCZ % NCY, rows % NCZ), columns, (NCX, NCY, NCZ))
        return jnp.dot(weights, moments, precision=highest, preferred_element_type=jnp.float32)
    local = lax.map(expand, jnp.arange(0, CELLS, block, dtype=jnp.int32)).reshape(CELLS, -1)
    coefficients = jnp.dot(local, translation, precision=highest, preferred_element_type=jnp.float32)
    coefficients = coefficients.reshape(NCX, NCY, NCZ, -1)
    return finish(lines, charge, mask, poly, near, coefficients, mobility, stress)
```

```python
import functools

import jax
import jax.numpy as jnp
from jax import lax
from jax.experimental import pallas as pl
from jax.experimental.pallas import tpu as pltpu
from jax.sharding import PartitionSpec as P

MESH = pl.DeviceIdType.MESH
core_square = 0.0625
near_scale = 0.01
slots = 128
terms = 35
term_rows = 40
source_rows = 40
split_rows = 32
f32, bf16 = jnp.float32, jnp.bfloat16

offsets_26 = [
    (x, y, z)
    for x in (-1, 0, 1)
    for y in (-1, 0, 1)
    for z in (-1, 0, 1)
    if (x, y, z) != (0, 0, 0)
]


def exponent_list():
    result = []
    for first in range(5):
        for second in range(5 - first):
            for third in range(5 - first - second):
                result.append((first, second, third))
    return result


def crossed(left, right):
    return [
        left[1] * right[2] - left[2] * right[1],
        left[2] * right[0] - left[0] * right[2],
        left[0] * right[1] - left[1] * right[0],
    ]


def high_low(value):
    high = value.astype(bf16).astype(f32)
    return high, value - high


def split_three(value):
    first, rest = high_low(value)
    second, rest = high_low(rest)
    return [first, second, rest.astype(bf16).astype(f32)]


def two_parts(value):
    high = value.astype(bf16)
    return high, (value - high.astype(f32)).astype(bf16)


def source_values(position, line, charge):
    pairs = [charge[a] * line[b] for a in range(3) for b in range(3)]
    projection = sum(charge[c] * position[c] for c in range(3))
    rows = list(pairs)
    for c in range(3):
        rows += [position[c] * value for value in pairs]
    rows += [projection * line[c] for c in range(3)]
    rows.append(jnp.zeros_like(projection))
    splits = []
    for c in range(3):
        first, second, third = split_three(position[c])
        splits += [first, first, first, second, second, third]
    splits += split_three(sum(position[c] * position[c] for c in range(3)))
    one = jnp.ones_like(projection)
    zero = jnp.zeros_like(projection)
    splits += [one] * 3 + [zero] * 8
    return rows, splits


def target_values(position, charge):
    squares = sum(position[c] * position[c] for c in range(3)) + core_square
    projection = sum(charge[c] * position[c] for c in range(3))
    zero = jnp.zeros_like(squares)
    one = jnp.ones_like(squares)
    distance, along = [], []
    for c in range(3):
        first, second, third = split_three(-2.0 * position[c])
        distance += [first, second, third, first, second, first]
        first, second, third = split_three(charge[c])
        along += [first, second, third, first, second, first]
    distance += [one] * 3 + split_three(squares) + [zero] * 8
    along += [zero] * 3 + split_three(-projection) + [zero] * 8
    return distance, along


def store_rows(ref, values, stride, first=0):
    for n, value in enumerate(values):
        ref[pl.ds(first + n, 8, stride=stride), :] = value


def eight_cells(halo, group, n):
    flat = halo.reshape(64 * 16, slots)
    return flat[pl.ds(group * 8 * 16 + n, 8, stride=16), :]


def pack_sources(stage_rows, stage_split, out_rows, out_split, first, first_split):
    for cell in range(8):
        value = stage_rows[pl.ds(cell * source_rows, source_rows), :]
        high, low = high_low(value)
        out_rows[first + cell] = jnp.concatenate([high, low], 0).astype(bf16)
    for half in range(2):
        value = stage_split[pl.ds(half * 4 * split_rows, 4 * split_rows), :]
        out_split[first_split + half] = value.T.astype(bf16)


def pair_weights(split, target):
    both = jnp.dot(split, target, preferred_element_type=f32)
    inverse = lax.rsqrt(both[:, :slots])
    square = inverse * inverse
    cube = square * inverse
    value = jnp.concatenate([cube, cube * square * both[:, slots:]], 1)
    return two_parts(value)


def summed(items):
    highs, lows, rows = [], [], []
    for split, target, row in items:
        high, low = pair_weights(split, target)
        highs.append(high)
        lows.append(low)
        rows.append(row)
    return jnp.dot(
        jnp.concatenate(rows + rows, 1),
        jnp.concatenate(highs + lows, 0),
        preferred_element_type=f32,
    )


def kernel(
    sizes,
    offsets_ref,
    lines_ref,
    burgers_ref,
    counts_ref,
    mobility_ref,
    stress_ref,
    translation_ref,
    out_ref,
    halo,
    gathered,
    partial,
    received,
    stage_rows,
    stage_split,
    stage_poly,
    local_rows,
    local_split,
    halo_rows,
    halo_split,
    target_rows,
    poly_rows,
    translation_rows,
    near_w,
    near_c,
    halo_send,
    halo_recv,
    line_send,
    line_recv,
):
    me = [lax.axis_index(name) for name in ("gx", "gy", "gz")]
    count_x, count_y, count_z = sizes

    def device(step_x, step_y, step_z):
        return tuple(
            lax.rem(me[axis] + step + sizes[axis], sizes[axis])
            for axis, step in enumerate((step_x, step_y, step_z))
        )

    partners = list(offsets_26)
    partners += [(u, 0, 0) for u in range(1, count_x) if u not in (1, count_x - 1)]
    partners += [(0, u, 0) for u in range(1, count_y) if u not in (1, count_y - 1)]
    partners += [(0, 0, u) for u in range(1, count_z) if u not in (1, count_z - 1)]
    barrier = pltpu.get_barrier_semaphore()
    for step in partners:
        pl.semaphore_signal(barrier, inc=1, device_id=device(*step), device_id_type=MESH)

    cell = lax.broadcasted_iota(jnp.int32, (8, slots), 0)
    lane = lax.broadcasted_iota(jnp.int32, (8, slots), 1)
    counts = jnp.zeros((8, slots), jnp.int32)
    mobility = jnp.zeros((8, slots), f32)
    for k in range(8):
        where = (k // 4, k // 2 % 2, k % 2)
        counts = jnp.where(cell == k, counts_ref[where], counts)
        mobility = jnp.where(cell == k, mobility_ref[where], mobility)
    mask = jnp.where(lane < counts, 1.0, 0.0).astype(f32)
    offsets = [offsets_ref[c] for c in range(3)]
    lines = [lines_ref[c] for c in range(3)]
    charge = [burgers_ref[c] * mask for c in range(3)]

    powers = []
    for base in offsets:
        square = base * base
        powers.append([jnp.ones_like(base), base, square, square * base, square * square])
    poly = []
    for first, second, third in exponent_list():
        factors = [powers[c][e] for c, e in enumerate((first, second, third)) if e]
        value = factors[0] if factors else powers[0][0]
        for factor in factors[1:]:
            value = value * factor
        poly.append(value)
    poly += [jnp.zeros((8, slots), f32)] * (term_rows - terms)
    store_rows(stage_poly, poly, term_rows)
    pad = jnp.zeros((slots - 2 * term_rows, slots), f32)
    for k in range(8):
        high, low = high_low(stage_poly[pl.ds(k * term_rows, term_rows), :])
        poly_rows[k] = jnp.concatenate([high, low, pad], 0).astype(bf16)
    dipole = crossed(charge, lines)
    highs, lows = [], []
    for value in dipole:
        high, low = high_low(value)
        highs.append(high)
        lows.append(low)
    zero = jnp.zeros((8, slots), f32)
    left = []
    for parts in (highs, lows):
        for k in range(8):
            rows = [jnp.where(cell == k, part, 0.0) for part in parts] + [zero]
            left.append(jnp.concatenate(rows, 0).astype(bf16))
    right = [poly_rows[k] for k in range(8)]
    moments = lax.dot_general(
        jnp.concatenate(left, 1),
        jnp.concatenate(right + right, 1),
        (((1,), (1,)), ((), ())),
        preferred_element_type=f32,
    )
    total = zero
    for m in range(3):
        part = moments[8 * m : 8 * m + 8]
        part = part + pltpu.roll(part, slots - term_rows, 1)
        part = jnp.where(lane < terms, part, 0.0)
        total = total + (part if m == 0 else pltpu.roll(part, terms * m, 1))
    gathered[0, 0] = total * (1.0 / slots)

    for c in range(3):
        for first, value in ((0, offsets), (3, lines), (6, charge)):
            for k in range(8):
                where = (1 + k // 4, 1 + k // 2 % 2, 1 + k % 2, pl.ds(first + c, 1))
                halo[where] = value[c][k : k + 1]

    pl.semaphore_wait(barrier, len(partners))

    def line_copy(axis, u, source, target):
        step = [0, 0, 0]
        step[axis] = u
        return pltpu.make_async_remote_copy(
            src_ref=source,
            dst_ref=target,
            send_sem=line_send.at[axis, u],
            recv_sem=line_recv.at[axis, u],
            device_id=device(*step),
            device_id_type=MESH,
        )

    copies_z = [
        line_copy(2, u, gathered.at[0, 0], gathered.at[0, u]) for u in range(1, count_z)
    ]
    for copy in copies_z:
        copy.start()
    sides = {
        -1: (pl.ds(1, 1), pl.ds(3, 1)),
        0: (pl.ds(1, 2), pl.ds(1, 2)),
        1: (pl.ds(2, 1), pl.ds(0, 1)),
    }
    copies_halo = []
    for n, step in enumerate(offsets_26):
        source = tuple(sides[s][0] for s in step)
        target = tuple(sides[s][1] for s in step)
        copies_halo.append(
            pltpu.make_async_remote_copy(
                src_ref=halo.at[source],
                dst_ref=halo.at[target],
                send_sem=halo_send.at[n],
                recv_sem=halo_recv.at[n],
                device_id=device(*step),
                device_id_type=MESH,
            )
        )
    for copy in copies_halo:
        copy.start()

    corner = [cell // 4, cell // 2 % 2, cell % 2]
    position = [offsets[c] + (corner[c].astype(f32) - 0.5) for c in range(3)]
    rows, splits = source_values(position, lines, charge)
    store_rows(stage_rows, rows, source_rows)
    store_rows(stage_split, splits, split_rows)
    pack_sources(stage_rows, stage_split, local_rows, local_split, 0, 0)
    distance, along = target_values(position, charge)
    target_rows[...] = jnp.zeros(target_rows.shape, bf16)
    for side, values in enumerate((distance, along)):
        store_rows(stage_split, values, split_rows)
        for k in range(8):
            value = stage_split[pl.ds(k * split_rows, split_rows), :].astype(bf16)
            for block in range(4):
                target_rows[
                    k, block, pl.ds(block * split_rows, split_rows), pl.ds(side * slots, slots)
                ] = value

    def near_local(k, _):
        items = []
        for source in range(8):
            items.append(
                (local_split[source // 4], target_rows[k, source % 4], local_rows[source])
            )
        value = summed(items)
        value = value[:source_rows] + value[source_rows:]
        near_w[pl.ds(pl.multiple_of(k * source_rows, 8), source_rows), :] = value[:, :slots]
        near_c[pl.ds(pl.multiple_of(k * source_rows, 8), source_rows), :] = value[:, slots:]
        return 0

    def near_halo(k, _):
        far_x, far_y, far_z = 3 * (k // 4), 3 * (k // 2 % 2), 3 * (k % 2)
        columns = [(x, y) for x in (1, 2, far_x) for y in (1, 2, far_y)]
        total = None
        group = []
        for n, (x, y) in enumerate(columns):
            remote = n not in (0, 1, 3, 4)
            for z in (1, 2, far_z) if remote else (far_z,):
                group.append(
                    (halo_split[4 * x + y], target_rows[k, z], halo_rows[16 * x + 4 * y + z])
                )
            if n in (2, 5, 6, 7, 8):
                value = summed(group)
                total = value if total is None else total + value
                group = []
        total = total[:source_rows] + total[source_rows:]
        where = pl.ds(pl.multiple_of(k * source_rows, 8), source_rows)
        near_w[where, :] += total[:, :slots]
        near_c[where, :] += total[:, slots:]
        return 0

    lax.fori_loop(0, 4, near_local, 0)
    for copy in copies_z:
        copy.wait()
    copies_y = [line_copy(1, u, gathered.at[0], gathered.at[u]) for u in range(1, count_y)]
    for copy in copies_y:
        copy.start()

    sources = count_y * count_z * 8
    target = lax.broadcasted_iota(jnp.int32, (count_x * 8, sources), 0)
    source = lax.broadcasted_iota(jnp.int32, (count_x * 8, sources), 1)
    apart = [
        2 * (target // 8) + target // 4 % 2 - source // 4 % 2,
        2 * (source // (8 * count_z)) + target // 2 % 2 - source // 2 % 2,
        2 * (source // 8 % count_z) + target % 2 - source % 2,
    ]
    largest, total_sq = 0, 0
    for axis in range(3):
        extent = 2 * sizes[axis]
        steps = lax.rem(apart[axis] + extent, extent)
        steps = jnp.minimum(steps, extent - steps)
        largest = jnp.maximum(largest, steps)
        total_sq = total_sq + steps * steps
    weights = jnp.where(largest > 1, lax.rsqrt(jnp.maximum(total_sq, 1).astype(f32)), 0.0)
    weights_high, weights_low = two_parts(weights)
    weights = jnp.concatenate([weights_high, weights_low, weights_high], 1)

    translation = translation_ref[...]
    for m in range(3):
        value = translation if m == 0 else pltpu.roll(translation, slots - terms * m, 1)
        value = jnp.where(lax.broadcasted_iota(jnp.int32, (slots, slots), 1) < terms, value, 0.0)
        high, low = two_parts(value)
        translation_rows[:, pl.ds(2 * m * slots, slots)] = high
        translation_rows[:, pl.ds((2 * m + 1) * slots, slots)] = low

    lax.fori_loop(4, 8, near_local, 0)

    for copy in copies_y:
        copy.wait()
    high, low = two_parts(gathered[...].reshape(sources, slots))
    partial[...] = jnp.dot(
        weights, jnp.concatenate([high, high, low], 0), preferred_element_type=f32
    ).reshape(count_x, 8, slots)
    copies_x = [line_copy(0, u, partial.at[u], received.at[u]) for u in range(1, count_x)]
    for copy in copies_x:
        copy.start()

    for copy in copies_halo:
        copy.wait()

    def prepare(group, _):
        value = [eight_cells(halo, group, n) for n in range(9)]
        place = [
            jnp.zeros((8, slots), jnp.int32) + group // 2,
            group % 2 * 2 + cell // 4,
            cell % 4,
        ]
        position = [value[c] + (place[c].astype(f32) - 1.5) for c in range(3)]
        rows, splits = source_values(position, value[3:6], value[6:9])
        store_rows(stage_rows, rows, source_rows)
        store_rows(stage_split, splits, split_rows)
        pack_sources(
            stage_rows, stage_split, halo_rows, halo_split, group * 8, group * 2
        )
        return 0

    lax.fori_loop(0, 8, prepare, 0)
    lax.fori_loop(0, 8, near_halo, 0)

    def row(ref, n):
        return ref[pl.ds(n, 8, stride=source_rows), :]

    pairs = [charge[a] * lines[b] for a in range(3) for b in range(3)]
    still = sum(pairs[n] * row(near_w, n) for n in range(9))
    near = []
    for c in range(3):
        first = sum(pairs[n] * row(near_w, 9 + 9 * c + n) for n in range(9))
        second = row(near_c, 36 + c) - sum(position[b] * row(near_c, 3 * b + c) for b in range(3))
        near.append(near_scale * (first - position[c] * still + second))

    for copy in copies_x:
        copy.wait()
    summed_moments = partial[0]
    for u in range(1, count_x):
        summed_moments = summed_moments + received[u]
    high, low = high_low(summed_moments)
    product = jnp.dot(
        jnp.concatenate([high, low], 0).astype(bf16),
        translation_rows[...],
        preferred_element_type=f32,
    )
    product = product[:8] + product[8:]
    highs, lows = [], []
    for m in range(3):
        value = product[:, 2 * m * slots : (2 * m + 1) * slots]
        value = value + product[:, (2 * m + 1) * slots : (2 * m + 2) * slots]
        for part, result in zip(high_low(value), (highs, lows)):
            result.append(part + pltpu.roll(part, term_rows, 1))
    left = [jnp.concatenate(parts + [zero], 0).astype(bf16) for parts in (highs, lows)]
    right = jnp.concatenate([poly_rows[k] for k in range(8)], 1)
    fields = jnp.dot(
        jnp.concatenate(left, 1),
        jnp.concatenate([right, right], 0),
        preferred_element_type=f32,
    )
    far = []
    for m in range(3):
        value = zero
        for k in range(8):
            value = jnp.where(
                cell == k, fields[8 * m : 8 * m + 8, k * slots : (k + 1) * slots], value
            )
        far.append(value * mask)

    stressed = [sum(stress_ref[a, b] * charge[b] for b in range(3)) for a in range(3)]
    applied = crossed(stressed, lines)
    force = [near[c] + far[c] + applied[c] for c in range(3)]
    along = sum(force[c] * lines[c] for c in range(3))
    along = along / jnp.maximum(sum(lines[c] * lines[c] for c in range(3)), 1.0)
    scale = mobility * mask
    for c in range(3):
        out_ref[c] = scale * (force[c] - along * lines[c])


def body(sizes, offsets, lines, burgers, counts, mobility, stress, translation):
    vmem, smem = (pl.BlockSpec(memory_space=space) for space in (pltpu.VMEM, pltpu.SMEM))
    shape = offsets.shape
    flat = (3, 8, slots)
    longest = max(sizes)
    result = pl.pallas_call(
        functools.partial(kernel, sizes),
        out_shape=jax.ShapeDtypeStruct(flat, f32),
        in_specs=[vmem, vmem, vmem, smem, smem, smem, vmem],
        out_specs=vmem,
        scratch_shapes=[
            pltpu.VMEM((4, 4, 4, 16, slots), f32),
            pltpu.VMEM((sizes[1], sizes[2], 8, slots), f32),
            pltpu.VMEM((sizes[0], 8, slots), f32),
            pltpu.VMEM((sizes[0], 8, slots), f32),
            pltpu.VMEM((8 * source_rows, slots), f32),
            pltpu.VMEM((8 * split_rows, slots), f32),
            pltpu.VMEM((8 * term_rows, slots), f32),
            pltpu.VMEM((8, 2 * source_rows, slots), bf16),
            pltpu.VMEM((2, slots, 4 * split_rows), bf16),
            pltpu.VMEM((64, 2 * source_rows, slots), bf16),
            pltpu.VMEM((16, slots, 4 * split_rows), bf16),
            pltpu.VMEM((8, 4, 4 * split_rows, 2 * slots), bf16),
            pltpu.VMEM((8, slots, slots), bf16),
            pltpu.VMEM((slots, 6 * slots), bf16),
            pltpu.VMEM((8 * source_rows, slots), f32),
            pltpu.VMEM((8 * source_rows, slots), f32),
            pltpu.SemaphoreType.DMA((26,)),
            pltpu.SemaphoreType.DMA((26,)),
            pltpu.SemaphoreType.DMA((3, longest)),
            pltpu.SemaphoreType.DMA((3, longest)),
        ],
        compiler_params=pltpu.CompilerParams(
            collective_id=0, has_side_effects=True, vmem_limit_bytes=48 * 1024 * 1024
        ),
    )(
        offsets.reshape(flat),
        lines.reshape(flat),
        burgers.reshape(flat),
        counts,
        mobility,
        stress,
        translation,
    )
    return result.reshape(shape)


def solution(mesh):
    sizes = tuple(mesh.shape[name] for name in ("gx", "gy", "gz"))
    placed = (
        P(None, "gx", "gy", "gz", None),
        P(None, "gx", "gy", "gz", None),
        P(None, "gx", "gy", "gz", None),
        P("gx", "gy", "gz"),
        P("gx", "gy", "gz"),
        P(),
        P(),
    )
    return jax.shard_map(
        functools.partial(body, sizes),
        mesh=mesh,
        in_specs=placed,
        out_specs=P(None, "gx", "gy", "gz", None),
        check_vma=False,
    )
```

```python
import functools

import jax
import jax.numpy as jnp
from jax import lax
from jax.experimental import pallas as pl
from jax.experimental.pallas import tpu as pltpu
from jax.sharding import PartitionSpec as P

MESH = pl.DeviceIdType.MESH
core_square = 0.0625
near_scale = 0.01
slots = 128
terms = 35
term_rows = 40
source_rows = 40
split_rows = 32
f32, bf16 = jnp.float32, jnp.bfloat16

offsets_26 = [
    (x, y, z)
    for x in (-1, 0, 1)
    for y in (-1, 0, 1)
    for z in (-1, 0, 1)
    if (x, y, z) != (0, 0, 0)
]


def exponent_list():
    result = []
    for first in range(5):
        for second in range(5 - first):
            for third in range(5 - first - second):
                result.append((first, second, third))
    return result


def crossed(left, right):
    return [
        left[1] * right[2] - left[2] * right[1],
        left[2] * right[0] - left[0] * right[2],
        left[0] * right[1] - left[1] * right[0],
    ]


def high_low(value):
    high = value.astype(bf16).astype(f32)
    return high, value - high


def split_three(value):
    first, rest = high_low(value)
    second, rest = high_low(rest)
    return [first, second, rest.astype(bf16).astype(f32)]


def two_parts(value):
    high = value.astype(bf16)
    return high, (value - high.astype(f32)).astype(bf16)


def source_values(position, line, charge):
    pairs = [charge[a] * line[b] for a in range(3) for b in range(3)]
    projection = sum(charge[c] * position[c] for c in range(3))
    rows = list(pairs)
    for c in range(3):
        rows += [position[c] * value for value in pairs]
    rows += [projection * line[c] for c in range(3)]
    rows.append(jnp.zeros_like(projection))
    splits = []
    for c in range(3):
        first, second, third = split_three(position[c])
        splits += [first, first, first, second, second, third]
    splits += split_three(sum(position[c] * position[c] for c in range(3)))
    one = jnp.ones_like(projection)
    zero = jnp.zeros_like(projection)
    splits += [one] * 3 + [zero] * 8
    return rows, splits


def target_values(position, charge):
    squares = sum(position[c] * position[c] for c in range(3)) + core_square
    projection = sum(charge[c] * position[c] for c in range(3))
    zero = jnp.zeros_like(squares)
    one = jnp.ones_like(squares)
    distance, along = [], []
    for c in range(3):
        first, second, third = split_three(-2.0 * position[c])
        distance += [first, second, third, first, second, first]
        first, second, third = split_three(charge[c])
        along += [first, second, third, first, second, first]
    distance += [one] * 3 + split_three(squares) + [zero] * 8
    along += [zero] * 3 + split_three(-projection) + [zero] * 8
    return distance, along


def store_rows(ref, values, stride, first=0):
    for n, value in enumerate(values):
        ref[pl.ds(first + n, 8, stride=stride), :] = value


def eight_cells(halo, group, n):
    flat = halo.reshape(64 * 16, slots)
    return flat[pl.ds(group * 8 * 16 + n, 8, stride=16), :]


def pack_sources(stage_rows, stage_split, out_rows, out_split, first, first_split):
    zero = jnp.zeros((source_rows, slots), f32)
    for cell in range(8):
        value = stage_rows[pl.ds(cell * source_rows, source_rows), :]
        high, low = high_low(value)
        out_rows[first + cell, :, pl.ds(0, slots)] = jnp.concatenate([high, low], 0).astype(bf16)
        out_rows[first + cell, :, pl.ds(slots, slots)] = jnp.concatenate([high, zero], 0).astype(
            bf16
        )
    for half in range(2):
        value = stage_split[pl.ds(half * 4 * split_rows, 4 * split_rows), :]
        out_split[first_split + half] = value.T.astype(bf16)


def product(pairs, unit=0, transpose=False):
    def scope(total):
        for n, (left, right) in enumerate(pairs):
            pltpu.matmul_push_rhs(right, n % 2, unit, transpose=transpose)
            pltpu.matmul_acc_lhs(total, left, load_staged_rhs=n % 2)
        return pltpu.matmul_pop(total)

    return pl.run_scoped(scope, pltpu.ACC(unit)((pairs[0][0].shape[0], 2 * slots), f32))


chunk = 32
chunks = slots // chunk
ahead = 4


def near_sums(blocks, plan, target_rows, store):
    count = len(blocks)
    held = next(n for n in range(ahead, 2 * ahead) if (count - ahead) % n == 0)

    def scope(total, *buffers):
        def buffer(p, n):
            return buffers[p % held * chunks + n]

        def start(p, k):
            first = p == 0 or blocks[p] != blocks[p - 1]
            block, splits, index, _, _ = plan(k, p)
            if first:
                rhs = target_rows[k, block]
                rhs = jnp.concatenate([rhs, jnp.zeros((slots, 2 * slots), bf16)], 0)
                pltpu.matmul_push_rhs(rhs, 0, 0)
            for n in range(chunks):
                left = splits[index, pl.ds(n * chunk, chunk), :]
                left = jnp.concatenate([left, jnp.zeros((chunk, slots), bf16)], 1)
                load = 0 if first and n == 0 else None
                pltpu.matmul_acc_lhs(buffer(p, n), left, load_staged_rhs=load)

        def finish(p, k):
            highs, lows = [], []
            for n in range(chunks):
                both = pltpu.matmul_pop(buffer(p, n))
                inverse = lax.rsqrt(both[:, :slots])
                square = inverse * inverse
                cube = square * inverse
                value = jnp.concatenate([cube, cube * square * both[:, slots:]], 1)
                high, low = two_parts(value)
                highs.append(high)
                lows.append(low)
            if p == 0:
                store(jnp.maximum(k - 1, 0), pltpu.matmul_pop(total))
            _, _, _, rows, place = plan(k, p)
            pltpu.matmul_push_rhs(jnp.concatenate(highs + lows, 0), p % 2, 1)
            pltpu.matmul_acc_lhs(total, rows[place], load_staged_rhs=p % 2)

        def target(k, _):
            for p in range(count):
                finish(p, k)
                if p + ahead < count:
                    start(p + ahead, k)
                else:
                    start(p + ahead - count, jnp.minimum(k + 1, 7))
            return 0

        for p in range(ahead):
            start(p, 0)
        lax.fori_loop(0, 8, target, 0)
        store(7, pltpu.matmul_pop(total))
        for p in range(ahead):
            for n in range(chunks):
                pltpu.matmul_pop(buffer(p, n))

    pl.run_scoped(
        scope,
        pltpu.ACC(1)((2 * source_rows, 2 * slots), f32),
        *[pltpu.ACC(0)((chunk, 2 * slots), f32)] * (held * chunks),
    )


def kernel(
    sizes,
    offsets_ref,
    lines_ref,
    burgers_ref,
    counts_ref,
    mobility_ref,
    stress_ref,
    translation_ref,
    out_ref,
    halo,
    gathered,
    partial,
    received,
    stage_rows,
    stage_split,
    stage_poly,
    local_rows,
    local_split,
    halo_rows,
    halo_split,
    target_rows,
    poly_rows,
    translation_rows,
    near_w,
    near_c,
    halo_w,
    halo_c,
    halo_send,
    halo_recv,
    line_send,
    line_recv,
):
    me = [lax.axis_index(name) for name in ("gx", "gy", "gz")]
    count_x, count_y, count_z = sizes

    def device(step_x, step_y, step_z):
        return tuple(
            lax.rem(me[axis] + step + sizes[axis], sizes[axis])
            for axis, step in enumerate((step_x, step_y, step_z))
        )

    partners = list(offsets_26)
    partners += [(u, 0, 0) for u in range(1, count_x) if u not in (1, count_x - 1)]
    partners += [(0, u, 0) for u in range(1, count_y) if u not in (1, count_y - 1)]
    partners += [(0, 0, u) for u in range(1, count_z) if u not in (1, count_z - 1)]
    barrier = pltpu.get_barrier_semaphore()
    for step in partners:
        pl.semaphore_signal(barrier, inc=1, device_id=device(*step), device_id_type=MESH)

    cell = lax.broadcasted_iota(jnp.int32, (8, slots), 0)
    lane = lax.broadcasted_iota(jnp.int32, (8, slots), 1)
    counts = jnp.zeros((8, slots), jnp.int32)
    mobility = jnp.zeros((8, slots), f32)
    for k in range(8):
        where = (k // 4, k // 2 % 2, k % 2)
        counts = jnp.where(cell == k, counts_ref[where], counts)
        mobility = jnp.where(cell == k, mobility_ref[where], mobility)
    mask = jnp.where(lane < counts, 1.0, 0.0).astype(f32)
    offsets = [offsets_ref[c] for c in range(3)]
    lines = [lines_ref[c] for c in range(3)]
    charge = [burgers_ref[c] * mask for c in range(3)]

    powers = []
    for base in offsets:
        square = base * base
        powers.append([jnp.ones_like(base), base, square, square * base, square * square])
    poly = []
    for first, second, third in exponent_list():
        factors = [powers[c][e] for c, e in enumerate((first, second, third)) if e]
        value = factors[0] if factors else powers[0][0]
        for factor in factors[1:]:
            value = value * factor
        poly.append(value)
    poly += [jnp.zeros((8, slots), f32)] * (term_rows - terms)
    store_rows(stage_poly, poly, term_rows)
    pad = jnp.zeros((slots - 2 * term_rows, slots), f32)
    for k in range(8):
        high, low = high_low(stage_poly[pl.ds(k * term_rows, term_rows), :])
        poly_rows[k] = jnp.concatenate([high, low, pad], 0).astype(bf16)
    dipole = crossed(charge, lines)
    highs, lows = [], []
    for value in dipole:
        high, low = high_low(value)
        highs.append(high)
        lows.append(low)
    zero = jnp.zeros((8, slots), f32)
    pairs = []
    for first in range(0, 8, 2):
        left = []
        for k in (first, first + 1):
            rows = [jnp.where(cell == k, part, 0.0) for part in highs] + [zero]
            rows += [jnp.where(cell == k, part, 0.0) for part in lows] + [zero]
            left.append(jnp.concatenate(rows, 0).astype(bf16))
        right = jnp.concatenate([poly_rows[first], poly_rows[first + 1]], 1)
        right = jnp.concatenate([right, jnp.zeros((slots, 2 * slots), bf16)], 0)
        pairs.append((jnp.concatenate(left, 1), right))
    moments = product(pairs, transpose=True)[:, :slots]
    moments = moments[:32] + moments[32:]
    total = zero
    for m in range(3):
        part = moments[8 * m : 8 * m + 8]
        part = part + pltpu.roll(part, slots - term_rows, 1)
        part = jnp.where(lane < terms, part, 0.0)
        total = total + (part if m == 0 else pltpu.roll(part, terms * m, 1))
    gathered[0, 0] = total * (1.0 / slots)

    for c in range(3):
        for first, value in ((0, offsets), (3, lines), (6, charge)):
            for k in range(8):
                where = (1 + k // 4, 1 + k // 2 % 2, 1 + k % 2, pl.ds(first + c, 1))
                halo[where] = value[c][k : k + 1]

    pl.semaphore_wait(barrier, len(partners))

    def line_copy(axis, u, source, target):
        step = [0, 0, 0]
        step[axis] = u
        return pltpu.make_async_remote_copy(
            src_ref=source,
            dst_ref=target,
            send_sem=line_send.at[axis, u],
            recv_sem=line_recv.at[axis, u],
            device_id=device(*step),
            device_id_type=MESH,
        )

    copies_z = [
        line_copy(2, u, gathered.at[0, 0], gathered.at[0, u]) for u in range(1, count_z)
    ]
    for copy in copies_z:
        copy.start()
    sides = {
        -1: (pl.ds(1, 1), pl.ds(3, 1)),
        0: (pl.ds(1, 2), pl.ds(1, 2)),
        1: (pl.ds(2, 1), pl.ds(0, 1)),
    }
    copies_halo = []
    for n, step in enumerate(offsets_26):
        source = tuple(sides[s][0] for s in step)
        target = tuple(sides[s][1] for s in step)
        copies_halo.append(
            pltpu.make_async_remote_copy(
                src_ref=halo.at[source],
                dst_ref=halo.at[target],
                send_sem=halo_send.at[n],
                recv_sem=halo_recv.at[n],
                device_id=device(*step),
                device_id_type=MESH,
            )
        )
    for copy in copies_halo:
        copy.start()

    corner = [cell // 4, cell // 2 % 2, cell % 2]
    position = [offsets[c] + (corner[c].astype(f32) - 0.5) for c in range(3)]
    rows, splits = source_values(position, lines, charge)
    store_rows(stage_rows, rows, source_rows)
    store_rows(stage_split, splits, split_rows)
    pack_sources(stage_rows, stage_split, local_rows, local_split, 0, 0)
    distance, along = target_values(position, charge)
    target_rows[...] = jnp.zeros(target_rows.shape, bf16)
    for side, values in enumerate((distance, along)):
        store_rows(stage_split, values, split_rows)
        for k in range(8):
            value = stage_split[pl.ds(k * split_rows, split_rows), :].astype(bf16)
            for block in range(4):
                target_rows[
                    k, block, pl.ds(block * split_rows, split_rows), pl.ds(side * slots, slots)
                ] = value

    local_order = [4 * half + place for place in range(4) for half in range(2)]

    def local_plan(k, p):
        source = local_order[p]
        return source % 4, local_split, source // 4, local_rows, source

    def keep(ref_w, ref_c, k, value):
        value = value[:source_rows] + value[source_rows:]
        where = pl.ds(pl.multiple_of(k * source_rows, 8), source_rows)
        ref_w[where, :] = value[:, :slots]
        ref_c[where, :] = value[:, slots:]

    halo_order = [(n, z) for z in range(3) for n in range(9) if z == 2 or n in (2, 5, 6, 7, 8)]

    def halo_plan(k, p):
        n, z = halo_order[p]
        x = (1, 2, 3 * (k // 4))[n // 3]
        y = (1, 2, 3 * (k // 2 % 2))[n % 3]
        z = (1, 2, 3 * (k % 2))[z]
        return z, halo_split, 4 * x + y, halo_rows, 16 * x + 4 * y + z

    def near_local():
        blocks = [source % 4 for source in local_order]
        near_sums(blocks, local_plan, target_rows, functools.partial(keep, near_w, near_c))

    def near_halo():
        blocks = [z for _, z in halo_order]
        near_sums(blocks, halo_plan, target_rows, functools.partial(keep, halo_w, halo_c))

    near_local()
    for copy in copies_z:
        copy.wait()
    copies_y = [line_copy(1, u, gathered.at[0], gathered.at[u]) for u in range(1, count_y)]
    for copy in copies_y:
        copy.start()

    sources = count_y * count_z * 8
    target = lax.broadcasted_iota(jnp.int32, (count_x * 8, sources), 0)
    source = lax.broadcasted_iota(jnp.int32, (count_x * 8, sources), 1)
    apart = [
        2 * (target // 8) + target // 4 % 2 - source // 4 % 2,
        2 * (source // (8 * count_z)) + target // 2 % 2 - source // 2 % 2,
        2 * (source // 8 % count_z) + target % 2 - source % 2,
    ]
    largest, total_sq = 0, 0
    for axis in range(3):
        extent = 2 * sizes[axis]
        steps = lax.rem(apart[axis] + extent, extent)
        steps = jnp.minimum(steps, extent - steps)
        largest = jnp.maximum(largest, steps)
        total_sq = total_sq + steps * steps
    weights = jnp.where(largest > 1, lax.rsqrt(jnp.maximum(total_sq, 1).astype(f32)), 0.0)
    weights = jnp.concatenate(two_parts(weights), 0)

    translation = translation_ref[...]
    for m in range(3):
        value = translation if m == 0 else pltpu.roll(translation, slots - terms * m, 1)
        value = jnp.where(lax.broadcasted_iota(jnp.int32, (slots, slots), 1) < terms, value, 0.0)
        high, low = two_parts(value)
        translation_rows[:, pl.ds(2 * m * slots, slots)] = high
        translation_rows[:, pl.ds((2 * m + 1) * slots, slots)] = low


    for copy in copies_y:
        copy.wait()
    right = jnp.concatenate(two_parts(gathered[...].reshape(sources, slots)), 1)
    value = product(
        [(weights[:, n : n + 256], right[n : n + 256]) for n in range(0, sources, 256)]
    )
    value = value[: 8 * count_x] + value[8 * count_x :]
    value = value[:, :slots] + value[:, slots:]
    partial[...] = value.reshape(count_x, 8, slots)
    copies_x = [line_copy(0, u, partial.at[u], received.at[u]) for u in range(1, count_x)]
    for copy in copies_x:
        copy.start()

    for copy in copies_halo:
        copy.wait()

    def prepare(group, _):
        value = [eight_cells(halo, group, n) for n in range(9)]
        place = [
            jnp.zeros((8, slots), jnp.int32) + group // 2,
            group % 2 * 2 + cell // 4,
            cell % 4,
        ]
        position = [value[c] + (place[c].astype(f32) - 1.5) for c in range(3)]
        rows, splits = source_values(position, value[3:6], value[6:9])
        store_rows(stage_rows, rows, source_rows)
        store_rows(stage_split, splits, split_rows)
        pack_sources(
            stage_rows, stage_split, halo_rows, halo_split, group * 8, group * 2
        )
        return 0

    lax.fori_loop(0, 8, prepare, 0)
    near_halo()

    def row(refs, n):
        return sum(ref[pl.ds(n, 8, stride=source_rows), :] for ref in refs)

    near_w, near_c = (near_w, halo_w), (near_c, halo_c)

    pairs = [charge[a] * lines[b] for a in range(3) for b in range(3)]
    still = sum(pairs[n] * row(near_w, n) for n in range(9))
    near = []
    for c in range(3):
        first = sum(pairs[n] * row(near_w, 9 + 9 * c + n) for n in range(9))
        second = row(near_c, 36 + c) - sum(position[b] * row(near_c, 3 * b + c) for b in range(3))
        near.append(near_scale * (first - position[c] * still + second))

    for copy in copies_x:
        copy.wait()
    summed_moments = partial[0]
    for u in range(1, count_x):
        summed_moments = summed_moments + received[u]
    high, low = high_low(summed_moments)
    left = jnp.concatenate([high, low], 0).astype(bf16)
    left = jnp.concatenate([left, jnp.zeros((16, slots), bf16)], 1)
    highs, lows = [], []
    for m in range(3):
        right = translation_rows[:, pl.ds(2 * m * slots, 2 * slots)]
        right = jnp.concatenate([right, jnp.zeros((slots, 2 * slots), bf16)], 0)
        value = product([(left, right)], m % 2)
        value = value[:8] + value[8:]
        value = value[:, :slots] + value[:, slots:]
        for part, result in zip(high_low(value), (highs, lows)):
            result.append(part + pltpu.roll(part, term_rows, 1))
    left = [jnp.concatenate(parts + [zero], 0).astype(bf16) for parts in (highs, lows)]
    left = jnp.concatenate(left, 1)
    far = [zero] * 3
    for first in range(0, 8, 2):
        right = jnp.concatenate([poly_rows[first], poly_rows[first + 1]], 1)
        fields = product([(left, jnp.concatenate([right, right], 0))], first // 2 % 2)
        for m in range(3):
            for n in range(2):
                field = fields[8 * m : 8 * m + 8, n * slots : (n + 1) * slots]
                far[m] = jnp.where(cell == first + n, field, far[m])
    far = [value * mask for value in far]

    stressed = [sum(stress_ref[a, b] * charge[b] for b in range(3)) for a in range(3)]
    applied = crossed(stressed, lines)
    force = [near[c] + far[c] + applied[c] for c in range(3)]
    along = sum(force[c] * lines[c] for c in range(3))
    along = along / jnp.maximum(sum(lines[c] * lines[c] for c in range(3)), 1.0)
    scale = mobility * mask
    for c in range(3):
        out_ref[c] = scale * (force[c] - along * lines[c])


def body(sizes, offsets, lines, burgers, counts, mobility, stress, translation):
    vmem, smem = (pl.BlockSpec(memory_space=space) for space in (pltpu.VMEM, pltpu.SMEM))
    shape = offsets.shape
    flat = (3, 8, slots)
    longest = max(sizes)
    result = pl.pallas_call(
        functools.partial(kernel, sizes),
        out_shape=jax.ShapeDtypeStruct(flat, f32),
        in_specs=[vmem, vmem, vmem, smem, smem, smem, vmem],
        out_specs=vmem,
        scratch_shapes=[
            pltpu.VMEM((4, 4, 4, 16, slots), f32),
            pltpu.VMEM((sizes[1], sizes[2], 8, slots), f32),
            pltpu.VMEM((sizes[0], 8, slots), f32),
            pltpu.VMEM((sizes[0], 8, slots), f32),
            pltpu.VMEM((8 * source_rows, slots), f32),
            pltpu.VMEM((8 * split_rows, slots), f32),
            pltpu.VMEM((8 * term_rows, slots), f32),
            pltpu.VMEM((8, 2 * source_rows, 2 * slots), bf16),
            pltpu.VMEM((2, slots, 4 * split_rows), bf16),
            pltpu.VMEM((64, 2 * source_rows, 2 * slots), bf16),
            pltpu.VMEM((16, slots, 4 * split_rows), bf16),
            pltpu.VMEM((8, 4, 4 * split_rows, 2 * slots), bf16),
            pltpu.VMEM((8, slots, slots), bf16),
            pltpu.VMEM((slots, 6 * slots), bf16),
            pltpu.VMEM((8 * source_rows, slots), f32),
            pltpu.VMEM((8 * source_rows, slots), f32),
            pltpu.VMEM((8 * source_rows, slots), f32),
            pltpu.VMEM((8 * source_rows, slots), f32),
            pltpu.SemaphoreType.DMA((26,)),
            pltpu.SemaphoreType.DMA((26,)),
            pltpu.SemaphoreType.DMA((3, longest)),
            pltpu.SemaphoreType.DMA((3, longest)),
        ],
        compiler_params=pltpu.CompilerParams(
            collective_id=0, has_side_effects=True, vmem_limit_bytes=48 * 1024 * 1024
        ),
    )(
        offsets.reshape(flat),
        lines.reshape(flat),
        burgers.reshape(flat),
        counts,
        mobility,
        stress,
        translation,
    )
    return result.reshape(shape)


def solution(mesh):
    sizes = tuple(mesh.shape[name] for name in ("gx", "gy", "gz"))
    placed = (
        P(None, "gx", "gy", "gz", None),
        P(None, "gx", "gy", "gz", None),
        P(None, "gx", "gy", "gz", None),
        P("gx", "gy", "gz"),
        P("gx", "gy", "gz"),
        P(),
        P(),
    )
    return jax.shard_map(
        functools.partial(body, sizes),
        mesh=mesh,
        in_specs=placed,
        out_specs=P(None, "gx", "gy", "gz", None),
        check_vma=False,
    )
```

```python
import functools

import jax
import jax.numpy as jnp
from jax import lax
from jax.experimental import pallas as pl
from jax.experimental.pallas import tpu as pltpu
from jax.sharding import PartitionSpec as P

MESH = pl.DeviceIdType.MESH
core_square = 0.0625
near_scale = 0.01
slots = 128
terms = 35
term_rows = 40
source_rows = 40
split_rows = 32
f32, bf16 = jnp.float32, jnp.bfloat16

offsets_26 = [
    (x, y, z)
    for x in (-1, 0, 1)
    for y in (-1, 0, 1)
    for z in (-1, 0, 1)
    if (x, y, z) != (0, 0, 0)
]


def exponent_list():
    result = []
    for first in range(5):
        for second in range(5 - first):
            for third in range(5 - first - second):
                result.append((first, second, third))
    return result


def crossed(left, right):
    return [
        left[1] * right[2] - left[2] * right[1],
        left[2] * right[0] - left[0] * right[2],
        left[0] * right[1] - left[1] * right[0],
    ]


def high_low(value):
    high = value.astype(bf16).astype(f32)
    return high, value - high


def split_three(value):
    first, rest = high_low(value)
    second, rest = high_low(rest)
    return [first, second, rest.astype(bf16).astype(f32)]


def two_parts(value):
    high = value.astype(bf16)
    return high, (value - high.astype(f32)).astype(bf16)


def source_values(position, line, charge):
    pairs = [charge[a] * line[b] for a in range(3) for b in range(3)]
    projection = sum(charge[c] * position[c] for c in range(3))
    rows = list(pairs)
    for c in range(3):
        rows += [position[c] * value for value in pairs]
    rows += [projection * line[c] for c in range(3)]
    rows.append(jnp.zeros_like(projection))
    splits = []
    for c in range(3):
        first, second, third = split_three(position[c])
        splits += [first, first, first, second, second, third]
    splits += split_three(sum(position[c] * position[c] for c in range(3)))
    one = jnp.ones_like(projection)
    zero = jnp.zeros_like(projection)
    splits += [one] * 3 + [zero] * 8
    return rows, splits


def target_values(position, charge):
    squares = sum(position[c] * position[c] for c in range(3)) + core_square
    projection = sum(charge[c] * position[c] for c in range(3))
    zero = jnp.zeros_like(squares)
    one = jnp.ones_like(squares)
    distance, along = [], []
    for c in range(3):
        first, second, third = split_three(-2.0 * position[c])
        distance += [first, second, third, first, second, first]
        first, second, third = split_three(charge[c])
        along += [first, second, third, first, second, first]
    distance += [one] * 3 + split_three(squares) + [zero] * 8
    along += [zero] * 3 + split_three(-projection) + [zero] * 8
    return distance, along


def store_rows(ref, values, stride, first=0):
    for n, value in enumerate(values):
        ref[pl.ds(first + n, 8, stride=stride), :] = value


def eight_cells(halo, group, n):
    flat = halo.reshape(64 * 16, slots)
    return flat[pl.ds(group * 8 * 16 + n, 8, stride=16), :]


def pack_sources(stage_rows, stage_split, out_rows, out_split, first, first_split):
    zero = jnp.zeros((source_rows, slots), f32)
    for cell in range(8):
        value = stage_rows[pl.ds(cell * source_rows, source_rows), :]
        high, low = high_low(value)
        out_rows[first + cell, :, pl.ds(0, slots)] = jnp.concatenate([high, low], 0).astype(bf16)
        out_rows[first + cell, :, pl.ds(slots, slots)] = jnp.concatenate([high, zero], 0).astype(
            bf16
        )
    for half in range(2):
        value = stage_split[pl.ds(half * 4 * split_rows, 4 * split_rows), :]
        out_split[first_split + half] = value.T.astype(bf16)


def products(groups, transpose=False):
    def scope(*totals):
        turn = [0, 0]
        for n, pairs in enumerate(groups):
            for left, right in pairs:
                staged = turn[n % 2] % 2
                turn[n % 2] += 1
                pltpu.matmul_push_rhs(right, staged, n % 2, transpose=transpose)
                pltpu.matmul_acc_lhs(totals[n], left, load_staged_rhs=staged)
        return [pltpu.matmul_pop(total) for total in totals]

    accumulators = [
        pltpu.ACC(n % 2)((pairs[0][0].shape[0], 2 * slots), f32) for n, pairs in enumerate(groups)
    ]
    return pl.run_scoped(scope, *accumulators)


chunk = 32
chunks = slots // chunk
ahead = 4


def near_sums(blocks, plan, target_rows, store):
    count = len(blocks)
    held = next(n for n in range(ahead, 2 * ahead) if (count - ahead) % n == 0)

    def scope(total, *buffers):
        def buffer(p, n):
            return buffers[p % held * chunks + n]

        def stage(p, k):
            block = plan(k, p)[0]
            rhs = jnp.concatenate([target_rows[k, block], jnp.zeros((slots, 2 * slots), bf16)], 0)
            pltpu.matmul_push_rhs(rhs, 0, 0)

        firsts = [p for p in range(count) if p == 0 or blocks[p] != blocks[p - 1]]

        def start(p, k, after):
            _, splits, index, _, _ = plan(k, p)
            for n in range(chunks):
                left = splits[index, pl.ds(n * chunk, chunk), :]
                left = jnp.concatenate([left, jnp.zeros((chunk, slots), bf16)], 1)
                load = 0 if p in firsts and n == 0 else None
                pltpu.matmul_acc_lhs(buffer(p, n), left, load_staged_rhs=load)
            if p in firsts:
                later = firsts.index(p) + 1
                if later < len(firsts):
                    stage(firsts[later], k)
                else:
                    stage(0, after)

        def finish(p, k):
            highs, lows = [], []
            for n in range(chunks):
                both = pltpu.matmul_pop(buffer(p, n))
                inverse = lax.rsqrt(both[:, :slots])
                square = inverse * inverse
                cube = square * inverse
                value = jnp.concatenate([cube, cube * square * both[:, slots:]], 1)
                high, low = two_parts(value)
                highs.append(high)
                lows.append(low)
            if p == 0:
                store(jnp.maximum(k - 1, 0), pltpu.matmul_pop(total))
            _, _, _, rows, place = plan(k, p)
            pltpu.matmul_push_rhs(jnp.concatenate(highs + lows, 0), p % 2, 1)
            pltpu.matmul_acc_lhs(total, rows[place], load_staged_rhs=p % 2)

        def target(k, _):
            after = jnp.minimum(k + 1, 7)
            for p in range(count):
                finish(p, k)
                if p + ahead < count:
                    start(p + ahead, k, after)
                else:
                    start(p + ahead - count, after, after)
            return 0

        stage(0, 0)
        for p in range(ahead):
            start(p, 0, 1)
        lax.fori_loop(0, 8, target, 0)
        store(7, pltpu.matmul_pop(total))
        pltpu.matmul_acc_lhs(
            buffer(0, 0), jnp.zeros((chunk, 2 * slots), bf16), load_staged_rhs=0
        )
        for p in range(ahead):
            for n in range(chunks):
                pltpu.matmul_pop(buffer(p, n))

    pl.run_scoped(
        scope,
        pltpu.ACC(1)((2 * source_rows, 2 * slots), f32),
        *[pltpu.ACC(0)((chunk, 2 * slots), f32)] * (held * chunks),
    )


def kernel(
    sizes,
    offsets_in,
    lines_in,
    burgers_in,
    counts_in,
    mobility_in,
    stress_in,
    translation_in,
    out_ref,
    offsets_ref,
    lines_ref,
    burgers_ref,
    counts_ref,
    mobility_ref,
    stress_ref,
    translation_ref,
    operand_sem,
    halo,
    gathered,
    partial,
    received,
    stage_rows,
    stage_split,
    stage_poly,
    local_rows,
    local_split,
    halo_rows,
    halo_split,
    target_rows,
    poly_rows,
    translation_rows,
    weight_rows,
    near_w,
    near_c,
    halo_w,
    halo_c,
    halo_send,
    halo_recv,
    gather_send,
    gather_recv,
    reduce_send,
    reduce_recv,
):
    operands = [
        (counts_in, counts_ref),
        (offsets_in, offsets_ref),
        (lines_in, lines_ref),
        (burgers_in, burgers_ref),
        (mobility_in, mobility_ref),
        (stress_in, stress_ref),
        (translation_in, translation_ref),
    ]
    loads = [
        pltpu.make_async_copy(source, target, operand_sem.at[n])
        for n, (source, target) in enumerate(operands)
    ]
    for load in loads:
        load.start()

    me = [lax.axis_index(name) for name in ("gx", "gy", "gz")]
    count_x, count_y, count_z = sizes

    def device(step_x, step_y, step_z):
        return tuple(
            lax.rem(me[axis] + step + sizes[axis], sizes[axis])
            for axis, step in enumerate((step_x, step_y, step_z))
        )

    chips = count_y // 2
    core = lax.rem(me[1], 2)
    over = 1 - 2 * core
    sources = [(r, b) for r in range(2) for b in range(count_z) if (r, b) != (0, 0)]
    goals = [(u, v) for u in range(count_x) for v in range(chips) if (u, v) != (0, 0)]
    partners = list(offsets_26)
    partners += [(0, r * over, b) for r, b in sources if b not in (0, 1, count_z - 1)]
    partners += [(u, 2 * v, 0) for u, v in goals if v or u not in (1, count_x - 1)]
    barrier = pltpu.get_barrier_semaphore()
    for step in partners:
        pl.semaphore_signal(barrier, inc=1, device_id=device(*step), device_id_type=MESH)

    shape = (count_x * chips * 8, 2 * count_z * 8)
    goal = lax.broadcasted_iota(jnp.int32, shape, 0)
    source = lax.broadcasted_iota(jnp.int32, shape, 1)
    apart = [
        2 * (goal // (8 * chips)) + goal // 4 % 2 - source // 4 % 2,
        4 * (goal // 8 % chips) - 2 * over * (source // (8 * count_z)) + goal // 2 % 2 - source // 2 % 2,
        2 * (source // 8 % count_z) + goal % 2 - source % 2,
    ]
    largest, total_sq = 0, 0
    for axis in range(3):
        extent = 2 * sizes[axis]
        steps = lax.rem(apart[axis] + extent, extent)
        steps = jnp.minimum(steps, extent - steps)
        largest = jnp.maximum(largest, steps)
        total_sq = total_sq + steps * steps
    weights = jnp.where(largest > 1, lax.rsqrt(jnp.maximum(total_sq, 1).astype(f32)), 0.0)
    weight_rows[...] = jnp.concatenate(two_parts(weights), 1)

    target_rows[...] = jnp.zeros(target_rows.shape, bf16)

    for load in loads[:4]:
        load.wait()
    cell = lax.broadcasted_iota(jnp.int32, (8, slots), 0)
    lane = lax.broadcasted_iota(jnp.int32, (8, slots), 1)
    counts = jnp.zeros((8, slots), jnp.int32)
    for k in range(8):
        where = (k // 4, k // 2 % 2, k % 2)
        counts = jnp.where(cell == k, counts_ref[where], counts)
    mask = jnp.where(lane < counts, 1.0, 0.0).astype(f32)
    offsets = [offsets_ref[c] for c in range(3)]
    lines = [lines_ref[c] for c in range(3)]
    charge = [burgers_ref[c] * mask for c in range(3)]

    powers = []
    for base in offsets:
        square = base * base
        powers.append([jnp.ones_like(base), base, square, square * base, square * square])
    poly = []
    for first, second, third in exponent_list():
        factors = [powers[c][e] for c, e in enumerate((first, second, third)) if e]
        value = factors[0] if factors else powers[0][0]
        for factor in factors[1:]:
            value = value * factor
        poly.append(value)
    poly += [jnp.zeros((8, slots), f32)] * (term_rows - terms)
    store_rows(stage_poly, poly, term_rows)
    pad = jnp.zeros((slots - 2 * term_rows, slots), f32)
    for k in range(8):
        high, low = high_low(stage_poly[pl.ds(k * term_rows, term_rows), :])
        poly_rows[k] = jnp.concatenate([high, low, pad], 0).astype(bf16)
    dipole = crossed(charge, lines)
    highs, lows = [], []
    for value in dipole:
        high, low = high_low(value)
        highs.append(high)
        lows.append(low)
    zero = jnp.zeros((8, slots), f32)
    pairs = []
    for first in range(0, 8, 2):
        left = []
        for k in (first, first + 1):
            rows = [jnp.where(cell == k, part, 0.0) for part in highs] + [zero]
            rows += [jnp.where(cell == k, part, 0.0) for part in lows] + [zero]
            left.append(jnp.concatenate(rows, 0).astype(bf16))
        right = jnp.concatenate([poly_rows[first], poly_rows[first + 1]], 1)
        right = jnp.concatenate([right, jnp.zeros((slots, 2 * slots), bf16)], 0)
        pairs.append((jnp.concatenate(left, 1), right))
    moments = sum(products([pairs[:2], pairs[2:]], transpose=True))[:, :slots]
    moments = moments[:32] + moments[32:]
    total = zero
    for m in range(3):
        part = moments[8 * m : 8 * m + 8]
        part = part + pltpu.roll(part, slots - term_rows, 1)
        part = jnp.where(lane < terms, part, 0.0)
        total = total + (part if m == 0 else pltpu.roll(part, terms * m, 1))
    gathered[0, 0] = total * (1.0 / slots)

    for c in range(3):
        for first, value in ((0, offsets), (3, lines), (6, charge)):
            for k in range(8):
                where = (1 + k // 4, 1 + k // 2 % 2, 1 + k % 2, pl.ds(first + c, 1))
                halo[where] = value[c][k : k + 1]

    pl.semaphore_wait(barrier, len(partners))

    copies_in = [
        pltpu.make_async_remote_copy(
            src_ref=gathered.at[0, 0],
            dst_ref=gathered.at[r, b],
            send_sem=gather_send.at[r, b],
            recv_sem=gather_recv.at[r, b],
            device_id=device(0, r * over, b),
            device_id_type=MESH,
        )
        for r, b in sources
    ]
    for copy in copies_in:
        copy.start()
    sides = {
        -1: (pl.ds(1, 1), pl.ds(3, 1)),
        0: (pl.ds(1, 2), pl.ds(1, 2)),
        1: (pl.ds(2, 1), pl.ds(0, 1)),
    }
    copies_halo = []
    for n, step in enumerate(offsets_26):
        source = tuple(sides[s][0] for s in step)
        target = tuple(sides[s][1] for s in step)
        copies_halo.append(
            pltpu.make_async_remote_copy(
                src_ref=halo.at[source],
                dst_ref=halo.at[target],
                send_sem=halo_send.at[n],
                recv_sem=halo_recv.at[n],
                device_id=device(*step),
                device_id_type=MESH,
            )
        )
    for copy in copies_halo:
        copy.start()

    corner = [cell // 4, cell // 2 % 2, cell % 2]
    position = [offsets[c] + (corner[c].astype(f32) - 0.5) for c in range(3)]
    rows, splits = source_values(position, lines, charge)
    store_rows(stage_rows, rows, source_rows)
    store_rows(stage_split, splits, split_rows)
    pack_sources(stage_rows, stage_split, local_rows, local_split, 0, 0)
    distance, along = target_values(position, charge)
    for side, values in enumerate((distance, along)):
        store_rows(stage_split, values, split_rows)
        for k in range(8):
            value = stage_split[pl.ds(k * split_rows, split_rows), :].astype(bf16)
            for block in range(4):
                target_rows[
                    k, block, pl.ds(block * split_rows, split_rows), pl.ds(side * slots, slots)
                ] = value

    local_order = [4 * half + place for place in range(4) for half in range(2)]

    def local_plan(k, p):
        source = local_order[p]
        return source % 4, local_split, source // 4, local_rows, source

    def keep(ref_w, ref_c, k, value):
        value = value[:source_rows] + value[source_rows:]
        where = pl.ds(pl.multiple_of(k * source_rows, 8), source_rows)
        ref_w[where, :] = value[:, :slots]
        ref_c[where, :] = value[:, slots:]

    halo_order = [(n, z) for z in range(3) for n in range(9) if z == 2 or n in (2, 5, 6, 7, 8)]

    def halo_plan(k, p):
        n, z = halo_order[p]
        x = (1, 2, 3 * (k // 4))[n // 3]
        y = (1, 2, 3 * (k // 2 % 2))[n % 3]
        z = (1, 2, 3 * (k % 2))[z]
        return z, halo_split, 4 * x + y, halo_rows, 16 * x + 4 * y + z

    def near_local():
        blocks = [source % 4 for source in local_order]
        near_sums(blocks, local_plan, target_rows, functools.partial(keep, near_w, near_c))

    def near_halo():
        blocks = [z for _, z in halo_order]
        near_sums(blocks, halo_plan, target_rows, functools.partial(keep, halo_w, halo_c))

    near_local()
    for load in loads[4:]:
        load.wait()
    mobility = jnp.zeros((8, slots), f32)
    for k in range(8):
        where = (k // 4, k // 2 % 2, k % 2)
        mobility = jnp.where(cell == k, mobility_ref[where], mobility)
    translation = translation_ref[...]
    for m in range(3):
        value = translation if m == 0 else pltpu.roll(translation, slots - terms * m, 1)
        value = jnp.where(lax.broadcasted_iota(jnp.int32, (slots, slots), 1) < terms, value, 0.0)
        high, low = two_parts(value)
        translation_rows[:, pl.ds(2 * m * slots, slots)] = high
        translation_rows[:, pl.ds((2 * m + 1) * slots, slots)] = low


    for copy in copies_in:
        copy.wait()
    high, low = two_parts(gathered[...].reshape(2 * count_z * 8, slots))
    both = jnp.concatenate([high, low], 1)
    both = jnp.concatenate([both, both], 0)
    half = weight_rows.shape[0] // 2
    values = products([[(weight_rows[pl.ds(n * half, half), :], both)] for n in range(2)])
    value = jnp.concatenate(values, 0)
    value = value[:, :slots] + value[:, slots:]
    partial[...] = value.reshape(count_x, chips, 8, slots)
    copies_out = [
        pltpu.make_async_remote_copy(
            src_ref=partial.at[u, v],
            dst_ref=received.at[u, v],
            send_sem=reduce_send.at[u, v],
            recv_sem=reduce_recv.at[u, v],
            device_id=device(u, 2 * v, 0),
            device_id_type=MESH,
        )
        for u, v in goals
    ]
    for copy in copies_out:
        copy.start()

    for copy in copies_halo:
        copy.wait()

    def prepare(group, _):
        value = [eight_cells(halo, group, n) for n in range(9)]
        place = [
            jnp.zeros((8, slots), jnp.int32) + group // 2,
            group % 2 * 2 + cell // 4,
            cell % 4,
        ]
        position = [value[c] + (place[c].astype(f32) - 1.5) for c in range(3)]
        rows, splits = source_values(position, value[3:6], value[6:9])
        store_rows(stage_rows, rows, source_rows)
        store_rows(stage_split, splits, split_rows)
        pack_sources(
            stage_rows, stage_split, halo_rows, halo_split, group * 8, group * 2
        )
        return 0

    lax.fori_loop(0, 8, prepare, 0)
    near_halo()

    def row(refs, n):
        return sum(ref[pl.ds(n, 8, stride=source_rows), :] for ref in refs)

    near_w, near_c = (near_w, halo_w), (near_c, halo_c)

    pairs = [charge[a] * lines[b] for a in range(3) for b in range(3)]
    still = sum(pairs[n] * row(near_w, n) for n in range(9))
    near = []
    for c in range(3):
        first = sum(pairs[n] * row(near_w, 9 + 9 * c + n) for n in range(9))
        second = row(near_c, 36 + c) - sum(position[b] * row(near_c, 3 * b + c) for b in range(3))
        near.append(near_scale * (first - position[c] * still + second))

    for copy in copies_out:
        copy.wait()
    received[0, 0] = partial[0, 0]
    summed_moments = jnp.sum(received[...].reshape(count_x * chips, 8, slots), 0)
    high, low = high_low(summed_moments)
    left = jnp.concatenate([high, low], 0).astype(bf16)
    left = jnp.concatenate([left, jnp.zeros((16, slots), bf16)], 1)
    groups = []
    for m in range(3):
        right = translation_rows[:, pl.ds(2 * m * slots, 2 * slots)]
        groups.append([(left, jnp.concatenate([right, jnp.zeros((slots, 2 * slots), bf16)], 0))])
    highs, lows = [], []
    for value in products(groups):
        value = value[:8] + value[8:]
        value = value[:, :slots] + value[:, slots:]
        for part, result in zip(high_low(value), (highs, lows)):
            result.append(part + pltpu.roll(part, term_rows, 1))
    left = [jnp.concatenate(parts + [zero], 0).astype(bf16) for parts in (highs, lows)]
    left = jnp.concatenate(left, 1)
    groups = []
    for first in range(0, 8, 2):
        right = jnp.concatenate([poly_rows[first], poly_rows[first + 1]], 1)
        groups.append([(left, jnp.concatenate([right, right], 0))])
    far = [zero] * 3
    for pair, fields in enumerate(products(groups)):
        for m in range(3):
            for n in range(2):
                field = fields[8 * m : 8 * m + 8, n * slots : (n + 1) * slots]
                far[m] = jnp.where(cell == 2 * pair + n, field, far[m])
    far = [value * mask for value in far]

    stressed = [sum(stress_ref[a, b] * charge[b] for b in range(3)) for a in range(3)]
    applied = crossed(stressed, lines)
    force = [near[c] + far[c] + applied[c] for c in range(3)]
    along = sum(force[c] * lines[c] for c in range(3))
    along = along / jnp.maximum(sum(lines[c] * lines[c] for c in range(3)), 1.0)
    scale = mobility * mask
    for c in range(3):
        out_ref[c] = scale * (force[c] - along * lines[c])


def body(sizes, offsets, lines, burgers, counts, mobility, stress, translation):
    vmem, hbm = (pl.BlockSpec(memory_space=space) for space in (pltpu.VMEM, pltpu.HBM))
    shape = offsets.shape
    flat = (3, 8, slots)
    chips = sizes[1] // 2
    result = pl.pallas_call(
        functools.partial(kernel, sizes),
        out_shape=jax.ShapeDtypeStruct(flat, f32),
        in_specs=[hbm] * 7,
        out_specs=vmem,
        scratch_shapes=[
            pltpu.VMEM(flat, f32),
            pltpu.VMEM(flat, f32),
            pltpu.VMEM(flat, f32),
            pltpu.SMEM(counts.shape, jnp.int32),
            pltpu.SMEM(mobility.shape, f32),
            pltpu.SMEM(stress.shape, f32),
            pltpu.VMEM(translation.shape, f32),
            pltpu.SemaphoreType.DMA((7,)),
            pltpu.VMEM((4, 4, 4, 16, slots), f32),
            pltpu.VMEM((2, sizes[2], 8, slots), f32),
            pltpu.VMEM((sizes[0], chips, 8, slots), f32),
            pltpu.VMEM((sizes[0], chips, 8, slots), f32),
            pltpu.VMEM((8 * source_rows, slots), f32),
            pltpu.VMEM((8 * split_rows, slots), f32),
            pltpu.VMEM((8 * term_rows, slots), f32),
            pltpu.VMEM((8, 2 * source_rows, 2 * slots), bf16),
            pltpu.VMEM((2, slots, 4 * split_rows), bf16),
            pltpu.VMEM((64, 2 * source_rows, 2 * slots), bf16),
            pltpu.VMEM((16, slots, 4 * split_rows), bf16),
            pltpu.VMEM((8, 4, 4 * split_rows, 2 * slots), bf16),
            pltpu.VMEM((8, slots, slots), bf16),
            pltpu.VMEM((slots, 6 * slots), bf16),
            pltpu.VMEM((sizes[0] * chips * 8, 4 * sizes[2] * 8), bf16),
            pltpu.VMEM((8 * source_rows, slots), f32),
            pltpu.VMEM((8 * source_rows, slots), f32),
            pltpu.VMEM((8 * source_rows, slots), f32),
            pltpu.VMEM((8 * source_rows, slots), f32),
            pltpu.SemaphoreType.DMA((26,)),
            pltpu.SemaphoreType.DMA((26,)),
            pltpu.SemaphoreType.DMA((2, sizes[2])),
            pltpu.SemaphoreType.DMA((2, sizes[2])),
            pltpu.SemaphoreType.DMA((sizes[0], chips)),
            pltpu.SemaphoreType.DMA((sizes[0], chips)),
        ],
        compiler_params=pltpu.CompilerParams(
            collective_id=0, has_side_effects=True, vmem_limit_bytes=60 * 1024 * 1024
        ),
    )(
        offsets.reshape(flat),
        lines.reshape(flat),
        burgers.reshape(flat),
        counts,
        mobility,
        stress,
        translation,
    )
    return result.reshape(shape)


def solution(mesh):
    sizes = tuple(mesh.shape[name] for name in ("gx", "gy", "gz"))
    placed = (
        P(None, "gx", "gy", "gz", None),
        P(None, "gx", "gy", "gz", None),
        P(None, "gx", "gy", "gz", None),
        P("gx", "gy", "gz"),
        P("gx", "gy", "gz"),
        P(),
        P(),
    )
    return jax.shard_map(
        functools.partial(body, sizes),
        mesh=mesh,
        in_specs=placed,
        out_specs=P(None, "gx", "gy", "gz", None),
        check_vma=False,
    )
```

```python
import functools

import jax
import jax.numpy as jnp
from jax import lax
from jax.experimental import pallas as pl
from jax.experimental.pallas import tpu as pltpu
from jax.sharding import PartitionSpec as P

MESH = pl.DeviceIdType.MESH
core_square = 0.0625
near_scale = 0.01
slots = 128
terms = 35
term_rows = 40
source_rows = 40
split_rows = 32
f32, bf16 = jnp.float32, jnp.bfloat16

offsets_26 = [
    (x, y, z)
    for x in (-1, 0, 1)
    for y in (-1, 0, 1)
    for z in (-1, 0, 1)
    if (x, y, z) != (0, 0, 0)
]


def exponent_list():
    result = []
    for first in range(5):
        for second in range(5 - first):
            for third in range(5 - first - second):
                result.append((first, second, third))
    return result


def crossed(left, right):
    return [
        left[1] * right[2] - left[2] * right[1],
        left[2] * right[0] - left[0] * right[2],
        left[0] * right[1] - left[1] * right[0],
    ]


def high_low(value):
    high = value.astype(bf16).astype(f32)
    return high, value - high


def split_three(value):
    first, rest = high_low(value)
    second, rest = high_low(rest)
    return [first, second, rest.astype(bf16).astype(f32)]


def two_parts(value):
    high = value.astype(bf16)
    return high, (value - high.astype(f32)).astype(bf16)


def source_values(position, line, charge):
    pairs = [charge[a] * line[b] for a in range(3) for b in range(3)]
    projection = sum(charge[c] * position[c] for c in range(3))
    rows = list(pairs)
    for c in range(3):
        rows += [position[c] * value for value in pairs]
    rows += [projection * line[c] for c in range(3)]
    rows.append(jnp.zeros_like(projection))
    splits = []
    for c in range(3):
        first, second, third = split_three(position[c])
        splits += [first, first, first, second, second, third]
    splits += split_three(sum(position[c] * position[c] for c in range(3)))
    one = jnp.ones_like(projection)
    zero = jnp.zeros_like(projection)
    splits += [one] * 3 + [zero] * 8
    return rows, splits


def target_values(position, charge):
    squares = sum(position[c] * position[c] for c in range(3)) + core_square
    projection = sum(charge[c] * position[c] for c in range(3))
    zero = jnp.zeros_like(squares)
    one = jnp.ones_like(squares)
    distance, along = [], []
    for c in range(3):
        first, second, third = split_three(-2.0 * position[c])
        distance += [first, second, third, first, second, first]
        first, second, third = split_three(charge[c])
        along += [first, second, third, first, second, first]
    distance += [one] * 3 + split_three(squares) + [zero] * 8
    along += [zero] * 3 + split_three(-projection) + [zero] * 8
    return distance, along


def store_rows(ref, values, stride, first=0):
    for n, value in enumerate(values):
        ref[pl.ds(first + n, 8, stride=stride), :] = value


def eight_cells(halo, group, n):
    flat = halo.reshape(64 * 16, slots)
    return flat[pl.ds(group * 8 * 16 + n, 8, stride=16), :]


def pack_sources(stage_rows, stage_split, out_rows, out_split, first, first_split, part=0):
    zero = jnp.zeros((source_rows, slots), f32)
    for cell in range(8):
        value = stage_rows[pl.ds((8 * part + cell) * source_rows, source_rows), :]
        high, low = high_low(value)
        out_rows[first + cell, :, pl.ds(0, slots)] = jnp.concatenate([high, low], 0).astype(bf16)
        out_rows[first + cell, :, pl.ds(slots, slots)] = jnp.concatenate([high, zero], 0).astype(
            bf16
        )
    for half in range(2):
        value = stage_split[pl.ds((2 * part + half) * 4 * split_rows, 4 * split_rows), :]
        out_split[first_split + half] = value.T.astype(bf16)


def products(groups, transpose=False):
    def scope(*totals):
        turn = [0, 0]
        for n, pairs in enumerate(groups):
            for left, right in pairs:
                staged = turn[n % 2] % 2
                turn[n % 2] += 1
                pltpu.matmul_push_rhs(right, staged, n % 2, transpose=transpose)
                pltpu.matmul_acc_lhs(totals[n], left, load_staged_rhs=staged)
        return [pltpu.matmul_pop(total) for total in totals]

    accumulators = [
        pltpu.ACC(n % 2)((pairs[0][0].shape[0], 2 * slots), f32) for n, pairs in enumerate(groups)
    ]
    return pl.run_scoped(scope, *accumulators)


chunk = 32
chunks = slots // chunk
ahead = 4


def near_sums(blocks, plan, target_rows, store):
    count = len(blocks)
    held = next(n for n in range(ahead, 2 * ahead) if (count - ahead) % n == 0)

    def scope(total, *buffers):
        def buffer(p, n):
            return buffers[p % held * chunks + n]

        def stage(p, k):
            block = plan(k, p)[0]
            rhs = jnp.concatenate([target_rows[k, block], jnp.zeros((slots, 2 * slots), bf16)], 0)
            pltpu.matmul_push_rhs(rhs, 0, 0)

        firsts = [p for p in range(count) if p == 0 or blocks[p] != blocks[p - 1]]

        def start(p, k, after):
            _, splits, index, _, _ = plan(k, p)
            for n in range(chunks):
                left = splits[index, pl.ds(n * chunk, chunk), :]
                left = jnp.concatenate([left, jnp.zeros((chunk, slots), bf16)], 1)
                load = 0 if p in firsts and n == 0 else None
                pltpu.matmul_acc_lhs(buffer(p, n), left, load_staged_rhs=load)
            if p in firsts:
                later = firsts.index(p) + 1
                if later < len(firsts):
                    stage(firsts[later], k)
                else:
                    stage(0, after)

        def finish(p, k):
            highs, lows = [], []
            for n in range(chunks):
                both = pltpu.matmul_pop(buffer(p, n))
                inverse = lax.rsqrt(both[:, :slots])
                square = inverse * inverse
                cube = square * inverse
                value = jnp.concatenate([cube, cube * square * both[:, slots:]], 1)
                high, low = two_parts(value)
                highs.append(high)
                lows.append(low)
            if p == 0:
                store(jnp.maximum(k - 1, 0), pltpu.matmul_pop(total))
            _, _, _, rows, place = plan(k, p)
            pltpu.matmul_push_rhs(jnp.concatenate(highs + lows, 0), p % 2, 1)
            pltpu.matmul_acc_lhs(total, rows[place], load_staged_rhs=p % 2)

        def target(k, _):
            after = jnp.minimum(k + 1, 7)
            for p in range(count):
                finish(p, k)
                if p + ahead < count:
                    start(p + ahead, k, after)
                else:
                    start(p + ahead - count, after, after)
            return 0

        stage(0, 0)
        for p in range(ahead):
            start(p, 0, 1)
        lax.fori_loop(0, 8, target, 0)
        store(7, pltpu.matmul_pop(total))
        pltpu.matmul_acc_lhs(
            buffer(0, 0), jnp.zeros((chunk, 2 * slots), bf16), load_staged_rhs=0
        )
        for p in range(ahead):
            for n in range(chunks):
                pltpu.matmul_pop(buffer(p, n))

    pl.run_scoped(
        scope,
        pltpu.ACC(1)((2 * source_rows, 2 * slots), f32),
        *[pltpu.ACC(0)((chunk, 2 * slots), f32)] * (held * chunks),
    )


def kernel(
    sizes,
    offsets_in,
    lines_in,
    burgers_in,
    counts_in,
    mobility_in,
    stress_in,
    translation_in,
    out_ref,
    offsets_ref,
    lines_ref,
    burgers_ref,
    counts_ref,
    mobility_ref,
    stress_ref,
    translation_ref,
    operand_sem,
    halo,
    gathered,
    partial,
    received,
    stage_rows,
    stage_split,
    stage_poly,
    local_rows,
    local_split,
    halo_rows,
    halo_split,
    target_rows,
    poly_rows,
    translation_rows,
    weight_rows,
    near_w,
    near_c,
    halo_w,
    halo_c,
    halo_send,
    halo_recv,
    gather_send,
    gather_recv,
    reduce_send,
    reduce_recv,
):
    operands = [
        (counts_in, counts_ref),
        (offsets_in, offsets_ref),
        (lines_in, lines_ref),
        (burgers_in, burgers_ref),
        (mobility_in, mobility_ref),
        (stress_in, stress_ref),
        (translation_in, translation_ref),
    ]
    loads = [
        pltpu.make_async_copy(source, target, operand_sem.at[n])
        for n, (source, target) in enumerate(operands)
    ]
    for load in loads:
        load.start()

    me = [lax.axis_index(name) for name in ("gx", "gy", "gz")]
    count_x, count_y, count_z = sizes

    def device(step_x, step_y, step_z):
        return tuple(
            lax.rem(me[axis] + step + sizes[axis], sizes[axis])
            for axis, step in enumerate((step_x, step_y, step_z))
        )

    chips = count_y // 2
    core = lax.rem(me[1], 2)
    over = 1 - 2 * core
    sources = [(r, b) for r in range(2) for b in range(count_z) if (r, b) != (0, 0)]
    goals = [(u, v) for u in range(count_x) for v in range(chips) if (u, v) != (0, 0)]
    partners = list(offsets_26)
    partners += [(0, r * over, b) for r, b in sources if b not in (0, 1, count_z - 1)]
    partners += [(u, 2 * v, 0) for u, v in goals if v or u not in (1, count_x - 1)]
    barrier = pltpu.get_barrier_semaphore()
    for step in partners:
        pl.semaphore_signal(barrier, inc=1, device_id=device(*step), device_id_type=MESH)

    shape = (count_x * chips * 8, 2 * count_z * 8)
    goal = lax.broadcasted_iota(jnp.int32, shape, 0)
    source = lax.broadcasted_iota(jnp.int32, shape, 1)
    apart = [
        2 * (goal // (8 * chips)) + goal // 4 % 2 - source // 4 % 2,
        4 * (goal // 8 % chips) - 2 * over * (source // (8 * count_z)) + goal // 2 % 2 - source // 2 % 2,
        2 * (source // 8 % count_z) + goal % 2 - source % 2,
    ]
    largest, total_sq = 0, 0
    for axis in range(3):
        extent = 2 * sizes[axis]
        steps = lax.rem(apart[axis] + extent, extent)
        steps = jnp.minimum(steps, extent - steps)
        largest = jnp.maximum(largest, steps)
        total_sq = total_sq + steps * steps
    weights = jnp.where(largest > 1, lax.rsqrt(jnp.maximum(total_sq, 1).astype(f32)), 0.0)
    weight_rows[...] = jnp.concatenate(two_parts(weights), 1)

    target_rows[...] = jnp.zeros(target_rows.shape, bf16)

    for load in loads[:4]:
        load.wait()
    cell = lax.broadcasted_iota(jnp.int32, (8, slots), 0)
    lane = lax.broadcasted_iota(jnp.int32, (8, slots), 1)
    counts = jnp.zeros((8, slots), jnp.int32)
    for k in range(8):
        where = (k // 4, k // 2 % 2, k % 2)
        counts = jnp.where(cell == k, counts_ref[where], counts)
    mask = jnp.where(lane < counts, 1.0, 0.0).astype(f32)
    offsets = [offsets_ref[c] for c in range(3)]
    lines = [lines_ref[c] for c in range(3)]
    charge = [burgers_ref[c] * mask for c in range(3)]

    powers = []
    for base in offsets:
        square = base * base
        powers.append([jnp.ones_like(base), base, square, square * base, square * square])
    poly = []
    for first, second, third in exponent_list():
        factors = [powers[c][e] for c, e in enumerate((first, second, third)) if e]
        value = factors[0] if factors else powers[0][0]
        for factor in factors[1:]:
            value = value * factor
        poly.append(value)
    poly += [jnp.zeros((8, slots), f32)] * (term_rows - terms)
    store_rows(stage_poly, poly, term_rows)
    pad = jnp.zeros((slots - 2 * term_rows, slots), f32)
    for k in range(8):
        high, low = high_low(stage_poly[pl.ds(k * term_rows, term_rows), :])
        poly_rows[k] = jnp.concatenate([high, low, pad], 0).astype(bf16)
    dipole = crossed(charge, lines)
    highs, lows = [], []
    for value in dipole:
        high, low = high_low(value)
        highs.append(high)
        lows.append(low)
    zero = jnp.zeros((8, slots), f32)
    pairs = []
    for first in range(0, 8, 2):
        left = []
        for k in (first, first + 1):
            rows = [jnp.where(cell == k, part, 0.0) for part in highs] + [zero]
            rows += [jnp.where(cell == k, part, 0.0) for part in lows] + [zero]
            left.append(jnp.concatenate(rows, 0).astype(bf16))
        right = jnp.concatenate([poly_rows[first], poly_rows[first + 1]], 1)
        right = jnp.concatenate([right, jnp.zeros((slots, 2 * slots), bf16)], 0)
        pairs.append((jnp.concatenate(left, 1), right))
    moments = sum(products([pairs[:2], pairs[2:]], transpose=True))[:, :slots]
    moments = moments[:32] + moments[32:]
    total = zero
    for m in range(3):
        part = moments[8 * m : 8 * m + 8]
        part = part + pltpu.roll(part, slots - term_rows, 1)
        part = jnp.where(lane < terms, part, 0.0)
        total = total + (part if m == 0 else pltpu.roll(part, terms * m, 1))
    gathered[0, 0] = total * (1.0 / slots)

    for c in range(3):
        for first, value in ((0, offsets), (3, lines), (6, charge)):
            for k in range(8):
                where = (1 + k // 4, 1 + k // 2 % 2, 1 + k % 2, pl.ds(first + c, 1))
                halo[where] = value[c][k : k + 1]

    pl.semaphore_wait(barrier, len(partners))

    copies_in = [
        pltpu.make_async_remote_copy(
            src_ref=gathered.at[0, 0],
            dst_ref=gathered.at[r, b],
            send_sem=gather_send.at[r, b],
            recv_sem=gather_recv.at[r, b],
            device_id=device(0, r * over, b),
            device_id_type=MESH,
        )
        for r, b in sources
    ]
    for copy in copies_in:
        copy.start()
    sides = {
        -1: (pl.ds(1, 1), pl.ds(3, 1)),
        0: (pl.ds(1, 2), pl.ds(1, 2)),
        1: (pl.ds(2, 1), pl.ds(0, 1)),
    }
    copies_halo = []
    for n, step in enumerate(offsets_26):
        source = tuple(sides[s][0] for s in step) + (pl.ds(0, 9),)
        target = tuple(sides[s][1] for s in step) + (pl.ds(0, 9),)
        copies_halo.append(
            pltpu.make_async_remote_copy(
                src_ref=halo.at[source],
                dst_ref=halo.at[target],
                send_sem=halo_send.at[n],
                recv_sem=halo_recv.at[n],
                device_id=device(*step),
                device_id_type=MESH,
            )
        )
    for copy in copies_halo:
        copy.start()

    corner = [cell // 4, cell // 2 % 2, cell % 2]
    position = [offsets[c] + (corner[c].astype(f32) - 0.5) for c in range(3)]
    rows, splits = source_values(position, lines, charge)
    store_rows(stage_rows, rows, source_rows)
    store_rows(stage_split, splits, split_rows)
    pack_sources(stage_rows, stage_split, local_rows, local_split, 0, 0)
    distance, along = target_values(position, charge)
    for side, values in enumerate((distance, along)):
        store_rows(stage_split, values, split_rows)
        for k in range(8):
            value = stage_split[pl.ds(k * split_rows, split_rows), :].astype(bf16)
            for block in range(4):
                target_rows[
                    k, block, pl.ds(block * split_rows, split_rows), pl.ds(side * slots, slots)
                ] = value

    local_order = [4 * half + place for place in range(4) for half in range(2)]

    def local_plan(k, p):
        source = local_order[p]
        return source % 4, local_split, source // 4, local_rows, source

    def keep(ref_w, ref_c, k, value):
        value = value[:source_rows] + value[source_rows:]
        where = pl.ds(pl.multiple_of(k * source_rows, 8), source_rows)
        ref_w[where, :] = value[:, :slots]
        ref_c[where, :] = value[:, slots:]

    halo_order = [(n, z) for z in range(3) for n in range(9) if z == 2 or n in (2, 5, 6, 7, 8)]

    def halo_plan(k, p):
        n, z = halo_order[p]
        x = (1, 2, 3 * (k // 4))[n // 3]
        y = (1, 2, 3 * (k // 2 % 2))[n % 3]
        z = (1, 2, 3 * (k % 2))[z]
        return z, halo_split, 4 * x + y, halo_rows, 16 * x + 4 * y + z

    def near_local():
        blocks = [source % 4 for source in local_order]
        near_sums(blocks, local_plan, target_rows, functools.partial(keep, near_w, near_c))

    def near_halo():
        blocks = [z for _, z in halo_order]
        near_sums(blocks, halo_plan, target_rows, functools.partial(keep, halo_w, halo_c))

    near_local()
    for load in loads[4:]:
        load.wait()
    mobility = jnp.zeros((8, slots), f32)
    for k in range(8):
        where = (k // 4, k // 2 % 2, k % 2)
        mobility = jnp.where(cell == k, mobility_ref[where], mobility)
    translation = translation_ref[...]
    for m in range(3):
        value = translation if m == 0 else pltpu.roll(translation, slots - terms * m, 1)
        value = jnp.where(lax.broadcasted_iota(jnp.int32, (slots, slots), 1) < terms, value, 0.0)
        high, low = two_parts(value)
        translation_rows[:, pl.ds(2 * m * slots, slots)] = high
        translation_rows[:, pl.ds((2 * m + 1) * slots, slots)] = low


    for copy in copies_in:
        copy.wait()
    high, low = two_parts(gathered[...].reshape(2 * count_z * 8, slots))
    both = jnp.concatenate([high, low], 1)
    both = jnp.concatenate([both, both], 0)
    half = weight_rows.shape[0] // 2
    values = products([[(weight_rows[pl.ds(n * half, half), :], both)] for n in range(2)])
    value = jnp.concatenate(values, 0)
    value = value[:, :slots] + value[:, slots:]
    partial[...] = value.reshape(count_x, chips, 8, slots)
    copies_out = [
        pltpu.make_async_remote_copy(
            src_ref=partial.at[u, v],
            dst_ref=received.at[u, v],
            send_sem=reduce_send.at[u, v],
            recv_sem=reduce_recv.at[u, v],
            device_id=device(u, 2 * v, 0),
            device_id_type=MESH,
        )
        for u, v in goals
    ]
    for copy in copies_out:
        copy.start()

    for copy in copies_halo:
        copy.wait()

    def prepare(pair, _):
        for half in range(2):
            group = 2 * pair + half
            value = [eight_cells(halo, group, n) for n in range(9)]
            place = [
                jnp.zeros((8, slots), jnp.int32) + pair,
                2 * half + cell // 4,
                cell % 4,
            ]
            position = [value[c] + (place[c].astype(f32) - 1.5) for c in range(3)]
            rows, splits = source_values(position, value[3:6], value[6:9])
            store_rows(stage_rows, rows, source_rows, 8 * source_rows * half)
            store_rows(stage_split, splits, split_rows, 8 * split_rows * half)
        for half in range(2):
            group = 2 * pair + half
            pack_sources(
                stage_rows, stage_split, halo_rows, halo_split, group * 8, group * 2, half
            )
        return 0

    lax.fori_loop(0, 4, prepare, 0)
    near_halo()

    def row(refs, n):
        return sum(ref[pl.ds(n, 8, stride=source_rows), :] for ref in refs)

    near_w, near_c = (near_w, halo_w), (near_c, halo_c)

    pairs = [charge[a] * lines[b] for a in range(3) for b in range(3)]
    still = sum(pairs[n] * row(near_w, n) for n in range(9))
    near = []
    for c in range(3):
        first = sum(pairs[n] * row(near_w, 9 + 9 * c + n) for n in range(9))
        second = row(near_c, 36 + c) - sum(position[b] * row(near_c, 3 * b + c) for b in range(3))
        near.append(near_scale * (first - position[c] * still + second))

    stressed = [sum(stress_ref[a, b] * charge[b] for b in range(3)) for a in range(3)]
    applied = crossed(stressed, lines)
    known = [near[c] + applied[c] for c in range(3)]
    shorten = 1.0 / jnp.maximum(sum(lines[c] * lines[c] for c in range(3)), 1.0)
    scale = mobility * mask

    for copy in copies_out:
        copy.wait()
    received[0, 0] = partial[0, 0]
    summed_moments = jnp.sum(received[...].reshape(count_x * chips, 8, slots), 0)
    high, low = high_low(summed_moments)
    left = jnp.concatenate([high, low], 0).astype(bf16)
    left = jnp.concatenate([left, jnp.zeros((16, slots), bf16)], 1)
    groups = []
    for m in range(3):
        right = translation_rows[:, pl.ds(2 * m * slots, 2 * slots)]
        groups.append([(left, jnp.concatenate([right, jnp.zeros((slots, 2 * slots), bf16)], 0))])
    highs, lows = [], []
    for value in products(groups):
        value = value[:8] + value[8:]
        value = value[:, :slots] + value[:, slots:]
        for part, result in zip(high_low(value), (highs, lows)):
            result.append(part + pltpu.roll(part, term_rows, 1))
    left = [jnp.concatenate(parts + [zero], 0).astype(bf16) for parts in (highs, lows)]
    left = jnp.concatenate(left, 1)
    groups = []
    for first in range(0, 8, 2):
        right = jnp.concatenate([poly_rows[first], poly_rows[first + 1]], 1)
        groups.append([(left, jnp.concatenate([right, right], 0))])
    far = [zero] * 3
    for pair, fields in enumerate(products(groups)):
        for m in range(3):
            for n in range(2):
                field = fields[8 * m : 8 * m + 8, n * slots : (n + 1) * slots]
                far[m] = jnp.where(cell == 2 * pair + n, field, far[m])
    far = [value * mask for value in far]

    force = [known[c] + far[c] for c in range(3)]
    along = sum(force[c] * lines[c] for c in range(3))
    along = along * shorten
    for c in range(3):
        out_ref[c] = scale * (force[c] - along * lines[c])


def body(sizes, offsets, lines, burgers, counts, mobility, stress, translation):
    vmem, hbm = (pl.BlockSpec(memory_space=space) for space in (pltpu.VMEM, pltpu.HBM))
    shape = offsets.shape
    flat = (3, 8, slots)
    chips = sizes[1] // 2
    result = pl.pallas_call(
        functools.partial(kernel, sizes),
        out_shape=jax.ShapeDtypeStruct(flat, f32),
        in_specs=[hbm] * 7,
        out_specs=vmem,
        scratch_shapes=[
            pltpu.VMEM(flat, f32),
            pltpu.VMEM(flat, f32),
            pltpu.VMEM(flat, f32),
            pltpu.SMEM(counts.shape, jnp.int32),
            pltpu.SMEM(mobility.shape, f32),
            pltpu.SMEM(stress.shape, f32),
            pltpu.VMEM(translation.shape, f32),
            pltpu.SemaphoreType.DMA((7,)),
            pltpu.VMEM((4, 4, 4, 16, slots), f32),
            pltpu.VMEM((2, sizes[2], 8, slots), f32),
            pltpu.VMEM((sizes[0], chips, 8, slots), f32),
            pltpu.VMEM((sizes[0], chips, 8, slots), f32),
            pltpu.VMEM((16 * source_rows, slots), f32),
            pltpu.VMEM((16 * split_rows, slots), f32),
            pltpu.VMEM((8 * term_rows, slots), f32),
            pltpu.VMEM((8, 2 * source_rows, 2 * slots), bf16),
            pltpu.VMEM((2, slots, 4 * split_rows), bf16),
            pltpu.VMEM((64, 2 * source_rows, 2 * slots), bf16),
            pltpu.VMEM((16, slots, 4 * split_rows), bf16),
            pltpu.VMEM((8, 4, 4 * split_rows, 2 * slots), bf16),
            pltpu.VMEM((8, slots, slots), bf16),
            pltpu.VMEM((slots, 6 * slots), bf16),
            pltpu.VMEM((sizes[0] * chips * 8, 4 * sizes[2] * 8), bf16),
            pltpu.VMEM((8 * source_rows, slots), f32),
            pltpu.VMEM((8 * source_rows, slots), f32),
            pltpu.VMEM((8 * source_rows, slots), f32),
            pltpu.VMEM((8 * source_rows, slots), f32),
            pltpu.SemaphoreType.DMA((26,)),
            pltpu.SemaphoreType.DMA((26,)),
            pltpu.SemaphoreType.DMA((2, sizes[2])),
            pltpu.SemaphoreType.DMA((2, sizes[2])),
            pltpu.SemaphoreType.DMA((sizes[0], chips)),
            pltpu.SemaphoreType.DMA((sizes[0], chips)),
        ],
        compiler_params=pltpu.CompilerParams(
            collective_id=0, has_side_effects=True, vmem_limit_bytes=60 * 1024 * 1024
        ),
    )(
        offsets.reshape(flat),
        lines.reshape(flat),
        burgers.reshape(flat),
        counts,
        mobility,
        stress,
        translation,
    )
    return result.reshape(shape)


def solution(mesh):
    sizes = tuple(mesh.shape[name] for name in ("gx", "gy", "gz"))
    placed = (
        P(None, "gx", "gy", "gz", None),
        P(None, "gx", "gy", "gz", None),
        P(None, "gx", "gy", "gz", None),
        P("gx", "gy", "gz"),
        P("gx", "gy", "gz"),
        P(),
        P(),
    )
    return jax.shard_map(
        functools.partial(body, sizes),
        mesh=mesh,
        in_specs=placed,
        out_specs=P(None, "gx", "gy", "gz", None),
        check_vma=False,
    )
```

```python
import functools

import jax
import jax.numpy as jnp
from jax import lax
from jax.experimental import pallas as pl
from jax.experimental.pallas import tpu as pltpu
from jax.sharding import PartitionSpec as P

MESH = pl.DeviceIdType.MESH
core_square = 0.0625
near_scale = 0.01
slots = 128
terms = 35
term_rows = 40
source_rows = 40
split_rows = 32
f32, bf16 = jnp.float32, jnp.bfloat16

offsets_26 = [
    (x, y, z)
    for x in (-1, 0, 1)
    for y in (-1, 0, 1)
    for z in (-1, 0, 1)
    if (x, y, z) != (0, 0, 0)
]


def exponent_list():
    result = []
    for first in range(5):
        for second in range(5 - first):
            for third in range(5 - first - second):
                result.append((first, second, third))
    return result


def crossed(left, right):
    return [
        left[1] * right[2] - left[2] * right[1],
        left[2] * right[0] - left[0] * right[2],
        left[0] * right[1] - left[1] * right[0],
    ]


def high_low(value):
    high = value.astype(bf16).astype(f32)
    return high, value - high


def split_three(value):
    first, rest = high_low(value)
    second, rest = high_low(rest)
    return [first, second, rest.astype(bf16).astype(f32)]


def two_parts(value):
    high = value.astype(bf16)
    return high, (value - high.astype(f32)).astype(bf16)


def source_values(position, line, charge):
    pairs = [charge[a] * line[b] for a in range(3) for b in range(3)]
    projection = sum(charge[c] * position[c] for c in range(3))
    rows = list(pairs)
    for c in range(3):
        rows += [position[c] * value for value in pairs]
    rows += [projection * line[c] for c in range(3)]
    rows.append(jnp.zeros_like(projection))
    splits = []
    for c in range(3):
        first, second, third = split_three(position[c])
        splits += [first, first, first, second, second, third]
    splits += split_three(sum(position[c] * position[c] for c in range(3)))
    one = jnp.ones_like(projection)
    zero = jnp.zeros_like(projection)
    splits += [one] * 3 + [zero] * 8
    return rows, splits


def target_values(position, charge):
    squares = sum(position[c] * position[c] for c in range(3)) + core_square
    projection = sum(charge[c] * position[c] for c in range(3))
    zero = jnp.zeros_like(squares)
    one = jnp.ones_like(squares)
    distance, along = [], []
    for c in range(3):
        first, second, third = split_three(-2.0 * position[c])
        distance += [first, second, third, first, second, first]
        first, second, third = split_three(charge[c])
        along += [first, second, third, first, second, first]
    distance += [one] * 3 + split_three(squares) + [zero] * 8
    along += [zero] * 3 + split_three(-projection) + [zero] * 8
    return distance, along


def store_rows(ref, values, stride, first=0):
    for n, value in enumerate(values):
        ref[pl.ds(first + n, 8, stride=stride), :] = value


def eight_cells(halo, group, n):
    flat = halo.reshape(64 * 16, slots)
    return flat[pl.ds(group * 8 * 16 + n, 8, stride=16), :]


def pack_sources(stage_rows, stage_split, out_rows, out_split, first, first_split, part=0):
    zero = jnp.zeros((source_rows, slots), f32)
    for cell in range(8):
        value = stage_rows[pl.ds((8 * part + cell) * source_rows, source_rows), :]
        high, low = high_low(value)
        out_rows[first + cell, :, pl.ds(0, slots)] = jnp.concatenate([high, low], 0).astype(bf16)
        out_rows[first + cell, :, pl.ds(slots, slots)] = jnp.concatenate([high, zero], 0).astype(
            bf16
        )
    for half in range(2):
        value = stage_split[pl.ds((2 * part + half) * 4 * split_rows, 4 * split_rows), :]
        out_split[first_split + half] = value.T.astype(bf16)


def products(groups, transpose=False):
    def scope(*totals):
        turn = [0, 0]
        for n, pairs in enumerate(groups):
            for left, right in pairs:
                staged = turn[n % 2] % 2
                turn[n % 2] += 1
                pltpu.matmul_push_rhs(right, staged, n % 2, transpose=transpose)
                pltpu.matmul_acc_lhs(totals[n], left, load_staged_rhs=staged)
        return [pltpu.matmul_pop(total) for total in totals]

    accumulators = [
        pltpu.ACC(n % 2)((pairs[0][0].shape[0], 2 * slots), f32) for n, pairs in enumerate(groups)
    ]
    return pl.run_scoped(scope, *accumulators)


chunk = 32
chunks = slots // chunk
ahead = 4


def near_sums(blocks, plan, target_rows, store, begin=0, end=8):
    count = len(blocks)
    held = next(n for n in range(ahead, 2 * ahead) if (count - ahead) % n == 0)

    def scope(total, *buffers):
        def buffer(p, n):
            return buffers[p % held * chunks + n]

        def stage(p, k):
            block = plan(k, p)[0]
            rhs = jnp.concatenate([target_rows[k, block], jnp.zeros((slots, 2 * slots), bf16)], 0)
            pltpu.matmul_push_rhs(rhs, 0, 0)

        firsts = [p for p in range(count) if p == 0 or blocks[p] != blocks[p - 1]]

        def start(p, k, after):
            _, splits, index, _, _ = plan(k, p)
            for n in range(chunks):
                left = splits[index, pl.ds(n * chunk, chunk), :]
                left = jnp.concatenate([left, jnp.zeros((chunk, slots), bf16)], 1)
                load = 0 if p in firsts and n == 0 else None
                pltpu.matmul_acc_lhs(buffer(p, n), left, load_staged_rhs=load)
            if p in firsts:
                later = firsts.index(p) + 1
                if later < len(firsts):
                    stage(firsts[later], k)
                else:
                    stage(0, after)

        def finish(p, k):
            highs, lows = [], []
            for n in range(chunks):
                both = pltpu.matmul_pop(buffer(p, n))
                inverse = lax.rsqrt(both[:, :slots])
                square = inverse * inverse
                cube = square * inverse
                value = jnp.concatenate([cube, cube * square * both[:, slots:]], 1)
                high, low = two_parts(value)
                highs.append(high)
                lows.append(low)
            if p == 0:
                store(jnp.maximum(k - 1, begin), pltpu.matmul_pop(total))
            _, _, _, rows, place = plan(k, p)
            pltpu.matmul_push_rhs(jnp.concatenate(highs + lows, 0), p % 2, 1)
            pltpu.matmul_acc_lhs(total, rows[place], load_staged_rhs=p % 2)

        def target(k, _):
            after = jnp.minimum(k + 1, end - 1)
            for p in range(count):
                finish(p, k)
                if p + ahead < count:
                    start(p + ahead, k, after)
                else:
                    start(p + ahead - count, after, after)
            return 0

        stage(0, begin)
        for p in range(ahead):
            start(p, begin, begin)
        lax.fori_loop(begin, end, target, 0)
        store(end - 1, pltpu.matmul_pop(total))
        pltpu.matmul_acc_lhs(
            buffer(0, 0), jnp.zeros((chunk, 2 * slots), bf16), load_staged_rhs=0
        )
        for p in range(ahead):
            for n in range(chunks):
                pltpu.matmul_pop(buffer(p, n))

    pl.run_scoped(
        scope,
        pltpu.ACC(1)((2 * source_rows, 2 * slots), f32),
        *[pltpu.ACC(0)((chunk, 2 * slots), f32)] * (held * chunks),
    )


def kernel(
    sizes,
    offsets_in,
    lines_in,
    burgers_in,
    counts_in,
    mobility_in,
    stress_in,
    translation_in,
    out_ref,
    offsets_ref,
    lines_ref,
    burgers_ref,
    counts_ref,
    mobility_ref,
    stress_ref,
    translation_ref,
    operand_sem,
    halo,
    gathered,
    partial,
    received,
    stage_rows,
    stage_split,
    stage_poly,
    local_rows,
    local_split,
    halo_rows,
    halo_split,
    target_rows,
    poly_rows,
    translation_rows,
    weight_rows,
    near_w,
    near_c,
    halo_w,
    halo_c,
    halo_send,
    halo_recv,
    gather_send,
    gather_recv,
    reduce_send,
    reduce_recv,
):
    operands = [
        (counts_in, counts_ref),
        (offsets_in, offsets_ref),
        (lines_in, lines_ref),
        (burgers_in, burgers_ref),
        (mobility_in, mobility_ref),
        (stress_in, stress_ref),
        (translation_in, translation_ref),
    ]
    loads = [
        pltpu.make_async_copy(source, target, operand_sem.at[n])
        for n, (source, target) in enumerate(operands)
    ]
    for load in loads:
        load.start()

    me = [lax.axis_index(name) for name in ("gx", "gy", "gz")]
    count_x, count_y, count_z = sizes

    def device(step_x, step_y, step_z):
        return tuple(
            lax.rem(me[axis] + step + sizes[axis], sizes[axis])
            for axis, step in enumerate((step_x, step_y, step_z))
        )

    chips = count_y // 2
    core = lax.rem(me[1], 2)
    over = 1 - 2 * core
    sources = [(r, b) for r in range(2) for b in range(count_z) if (r, b) != (0, 0)]
    goals = [(u, v) for u in range(count_x) for v in range(chips) if (u, v) != (0, 0)]
    partners = list(offsets_26)
    partners += [(0, r * over, b) for r, b in sources if b not in (0, 1, count_z - 1)]
    partners += [(u, 2 * v, 0) for u, v in goals if v or u not in (1, count_x - 1)]
    barrier = pltpu.get_barrier_semaphore()
    for step in partners:
        pl.semaphore_signal(barrier, inc=1, device_id=device(*step), device_id_type=MESH)

    target_rows[...] = jnp.zeros(target_rows.shape, bf16)

    for load in loads[:4]:
        load.wait()
    cell = lax.broadcasted_iota(jnp.int32, (8, slots), 0)
    lane = lax.broadcasted_iota(jnp.int32, (8, slots), 1)
    counts = jnp.zeros((8, slots), jnp.int32)
    for k in range(8):
        where = (k // 4, k // 2 % 2, k % 2)
        counts = jnp.where(cell == k, counts_ref[where], counts)
    mask = jnp.where(lane < counts, 1.0, 0.0).astype(f32)
    offsets = [offsets_ref[c] for c in range(3)]
    lines = [lines_ref[c] for c in range(3)]
    charge = [burgers_ref[c] * mask for c in range(3)]

    powers = []
    for base in offsets:
        square = base * base
        powers.append([jnp.ones_like(base), base, square, square * base, square * square])
    poly = []
    for first, second, third in exponent_list():
        factors = [powers[c][e] for c, e in enumerate((first, second, third)) if e]
        value = factors[0] if factors else powers[0][0]
        for factor in factors[1:]:
            value = value * factor
        poly.append(value)
    poly += [jnp.zeros((8, slots), f32)] * (term_rows - terms)
    store_rows(stage_poly, poly, term_rows)
    pad = jnp.zeros((slots - 2 * term_rows, slots), f32)
    for k in range(8):
        high, low = high_low(stage_poly[pl.ds(k * term_rows, term_rows), :])
        poly_rows[k] = jnp.concatenate([high, low, pad], 0).astype(bf16)
    dipole = crossed(charge, lines)
    highs, lows = [], []
    for value in dipole:
        high, low = high_low(value)
        highs.append(high)
        lows.append(low)
    zero = jnp.zeros((8, slots), f32)
    pairs = []
    for first in range(0, 8, 2):
        left = []
        for k in (first, first + 1):
            rows = [jnp.where(cell == k, part, 0.0) for part in highs] + [zero]
            rows += [jnp.where(cell == k, part, 0.0) for part in lows] + [zero]
            left.append(jnp.concatenate(rows, 0).astype(bf16))
        right = jnp.concatenate([poly_rows[first], poly_rows[first + 1]], 1)
        right = jnp.concatenate([right, jnp.zeros((slots, 2 * slots), bf16)], 0)
        pairs.append((jnp.concatenate(left, 1), right))
    moments = sum(products([pairs[:2], pairs[2:]], transpose=True))[:, :slots]
    moments = moments[:32] + moments[32:]
    total = zero
    for m in range(3):
        part = moments[8 * m : 8 * m + 8]
        part = part + pltpu.roll(part, slots - term_rows, 1)
        part = jnp.where(lane < terms, part, 0.0)
        total = total + (part if m == 0 else pltpu.roll(part, terms * m, 1))
    gathered[0, 0] = total * (1.0 / slots)

    for c in range(3):
        for first, value in ((0, offsets), (3, lines), (6, charge)):
            for k in range(8):
                where = (1 + k // 4, 1 + k // 2 % 2, 1 + k % 2, pl.ds(first + c, 1))
                halo[where] = value[c][k : k + 1]

    pl.semaphore_wait(barrier, len(partners))

    copies_in = [
        pltpu.make_async_remote_copy(
            src_ref=gathered.at[0, 0],
            dst_ref=gathered.at[r, b],
            send_sem=gather_send.at[r, b],
            recv_sem=gather_recv.at[r, b],
            device_id=device(0, r * over, b),
            device_id_type=MESH,
        )
        for r, b in sources
    ]
    for copy in copies_in:
        copy.start()
    sides = {
        -1: (pl.ds(1, 1), pl.ds(3, 1)),
        0: (pl.ds(1, 2), pl.ds(1, 2)),
        1: (pl.ds(2, 1), pl.ds(0, 1)),
    }
    copies_halo = []
    for n, step in enumerate(offsets_26):
        source = tuple(sides[s][0] for s in step) + (pl.ds(0, 9),)
        target = tuple(sides[s][1] for s in step) + (pl.ds(0, 9),)
        copies_halo.append(
            pltpu.make_async_remote_copy(
                src_ref=halo.at[source],
                dst_ref=halo.at[target],
                send_sem=halo_send.at[n],
                recv_sem=halo_recv.at[n],
                device_id=device(*step),
                device_id_type=MESH,
            )
        )
    for copy in copies_halo:
        copy.start()

    corner = [cell // 4, cell // 2 % 2, cell % 2]
    position = [offsets[c] + (corner[c].astype(f32) - 0.5) for c in range(3)]
    rows, splits = source_values(position, lines, charge)
    store_rows(stage_rows, rows, source_rows)
    store_rows(stage_split, splits, split_rows)
    pack_sources(stage_rows, stage_split, local_rows, local_split, 0, 0)
    distance, along = target_values(position, charge)
    for side, values in enumerate((distance, along)):
        store_rows(stage_split, values, split_rows)
        for k in range(8):
            value = stage_split[pl.ds(k * split_rows, split_rows), :].astype(bf16)
            for block in range(4):
                target_rows[
                    k, block, pl.ds(block * split_rows, split_rows), pl.ds(side * slots, slots)
                ] = value

    local_order = [4 * half + place for place in range(4) for half in range(2)]

    def local_plan(k, p):
        source = local_order[p]
        return source % 4, local_split, source // 4, local_rows, source

    def keep(ref_w, ref_c, k, value):
        value = value[:source_rows] + value[source_rows:]
        where = pl.ds(pl.multiple_of(k * source_rows, 8), source_rows)
        ref_w[where, :] = value[:, :slots]
        ref_c[where, :] = value[:, slots:]

    halo_order = [(n, z) for z in range(3) for n in range(9) if z == 2 or n in (2, 5, 6, 7, 8)]

    def halo_plan(k, p):
        n, z = halo_order[p]
        x = (1, 2, 3 * (k // 4))[n // 3]
        y = (1, 2, 3 * (k // 2 % 2))[n % 3]
        z = (1, 2, 3 * (k % 2))[z]
        return z, halo_split, 4 * x + y, halo_rows, 16 * x + 4 * y + z

    def near_local(begin, end):
        blocks = [source % 4 for source in local_order]
        keep_local = functools.partial(keep, near_w, near_c)
        near_sums(blocks, local_plan, target_rows, keep_local, begin, end)

    def near_halo():
        blocks = [z for _, z in halo_order]
        near_sums(blocks, halo_plan, target_rows, functools.partial(keep, halo_w, halo_c))

    shape = (count_x * chips * 8, 2 * count_z * 8)
    goal = lax.broadcasted_iota(jnp.int32, shape, 0)
    source = lax.broadcasted_iota(jnp.int32, shape, 1)
    apart = [
        2 * (goal // (8 * chips)) + goal // 4 % 2 - source // 4 % 2,
        4 * (goal // 8 % chips) - 2 * over * (source // (8 * count_z)) + goal // 2 % 2 - source // 2 % 2,
        2 * (source // 8 % count_z) + goal % 2 - source % 2,
    ]
    largest, total_sq = 0, 0
    for axis in range(3):
        extent = 2 * sizes[axis]
        steps = lax.rem(apart[axis] + extent, extent)
        steps = jnp.minimum(steps, extent - steps)
        largest = jnp.maximum(largest, steps)
        total_sq = total_sq + steps * steps
    weights = jnp.where(largest > 1, lax.rsqrt(jnp.maximum(total_sq, 1).astype(f32)), 0.0)
    weight_rows[...] = jnp.concatenate(two_parts(weights), 1)

    near_local(0, 8)
    for load in loads[4:]:
        load.wait()
    mobility = jnp.zeros((8, slots), f32)
    for k in range(8):
        where = (k // 4, k // 2 % 2, k % 2)
        mobility = jnp.where(cell == k, mobility_ref[where], mobility)
    translation = translation_ref[...]
    for m in range(3):
        value = translation if m == 0 else pltpu.roll(translation, slots - terms * m, 1)
        value = jnp.where(lax.broadcasted_iota(jnp.int32, (slots, slots), 1) < terms, value, 0.0)
        high, low = two_parts(value)
        translation_rows[:, pl.ds(2 * m * slots, slots)] = high
        translation_rows[:, pl.ds((2 * m + 1) * slots, slots)] = low


    for copy in copies_in:
        copy.wait()
    high, low = two_parts(gathered[...].reshape(2 * count_z * 8, slots))
    both = jnp.concatenate([high, low], 1)
    both = jnp.concatenate([both, both], 0)
    half = weight_rows.shape[0] // 2
    values = products([[(weight_rows[pl.ds(n * half, half), :], both)] for n in range(2)])
    value = jnp.concatenate(values, 0)
    value = value[:, :slots] + value[:, slots:]
    partial[...] = value.reshape(count_x, chips, 8, slots)
    copies_out = [
        pltpu.make_async_remote_copy(
            src_ref=partial.at[u, v],
            dst_ref=received.at[u, v],
            send_sem=reduce_send.at[u, v],
            recv_sem=reduce_recv.at[u, v],
            device_id=device(u, 2 * v, 0),
            device_id_type=MESH,
        )
        for u, v in goals
    ]
    for copy in copies_out:
        copy.start()

    for copy in copies_halo:
        copy.wait()

    def prepare(pair, _):
        for half in range(2):
            group = 2 * pair + half
            value = [eight_cells(halo, group, n) for n in range(9)]
            place = [
                jnp.zeros((8, slots), jnp.int32) + pair,
                2 * half + cell // 4,
                cell % 4,
            ]
            position = [value[c] + (place[c].astype(f32) - 1.5) for c in range(3)]
            rows, splits = source_values(position, value[3:6], value[6:9])
            store_rows(stage_rows, rows, source_rows, 8 * source_rows * half)
            store_rows(stage_split, splits, split_rows, 8 * split_rows * half)
        for half in range(2):
            group = 2 * pair + half
            pack_sources(
                stage_rows, stage_split, halo_rows, halo_split, group * 8, group * 2, half
            )
        return 0

    lax.fori_loop(0, 4, prepare, 0)
    near_halo()

    def row(refs, n):
        return sum(ref[pl.ds(n, 8, stride=source_rows), :] for ref in refs)

    near_w, near_c = (near_w, halo_w), (near_c, halo_c)

    pairs = [charge[a] * lines[b] for a in range(3) for b in range(3)]
    still = sum(pairs[n] * row(near_w, n) for n in range(9))
    near = []
    for c in range(3):
        first = sum(pairs[n] * row(near_w, 9 + 9 * c + n) for n in range(9))
        second = row(near_c, 36 + c) - sum(position[b] * row(near_c, 3 * b + c) for b in range(3))
        near.append(near_scale * (first - position[c] * still + second))

    stressed = [sum(stress_ref[a, b] * charge[b] for b in range(3)) for a in range(3)]
    applied = crossed(stressed, lines)
    known = [near[c] + applied[c] for c in range(3)]
    shorten = 1.0 / jnp.maximum(sum(lines[c] * lines[c] for c in range(3)), 1.0)
    scale = mobility * mask

    for copy in copies_out:
        copy.wait()
    received[0, 0] = partial[0, 0]
    summed_moments = jnp.sum(received[...].reshape(count_x * chips, 8, slots), 0)
    high, low = high_low(summed_moments)
    left = jnp.concatenate([high, low], 0).astype(bf16)
    left = jnp.concatenate([left, jnp.zeros((16, slots), bf16)], 1)
    groups = []
    for m in range(3):
        right = translation_rows[:, pl.ds(2 * m * slots, 2 * slots)]
        groups.append([(left, jnp.concatenate([right, jnp.zeros((slots, 2 * slots), bf16)], 0))])
    highs, lows = [], []
    for value in products(groups):
        value = value[:8] + value[8:]
        value = value[:, :slots] + value[:, slots:]
        for part, result in zip(high_low(value), (highs, lows)):
            result.append(part + pltpu.roll(part, term_rows, 1))
    left = [jnp.concatenate(parts + [zero], 0).astype(bf16) for parts in (highs, lows)]
    left = jnp.concatenate(left, 1)
    groups = []
    for first in range(0, 8, 2):
        right = jnp.concatenate([poly_rows[first], poly_rows[first + 1]], 1)
        groups.append([(left, jnp.concatenate([right, right], 0))])
    far = [zero] * 3
    for pair, fields in enumerate(products(groups)):
        for m in range(3):
            for n in range(2):
                field = fields[8 * m : 8 * m + 8, n * slots : (n + 1) * slots]
                far[m] = jnp.where(cell == 2 * pair + n, field, far[m])
    far = [value * mask for value in far]

    force = [known[c] + far[c] for c in range(3)]
    along = sum(force[c] * lines[c] for c in range(3))
    along = along * shorten
    for c in range(3):
        out_ref[c] = scale * (force[c] - along * lines[c])


def body(sizes, offsets, lines, burgers, counts, mobility, stress, translation):
    vmem, hbm = (pl.BlockSpec(memory_space=space) for space in (pltpu.VMEM, pltpu.HBM))
    shape = offsets.shape
    flat = (3, 8, slots)
    chips = sizes[1] // 2
    result = pl.pallas_call(
        functools.partial(kernel, sizes),
        out_shape=pltpu.VMEM(flat, f32),
        in_specs=[hbm] * 7,
        out_specs=vmem,
        scratch_shapes=[
            pltpu.VMEM(flat, f32),
            pltpu.VMEM(flat, f32),
            pltpu.VMEM(flat, f32),
            pltpu.SMEM(counts.shape, jnp.int32),
            pltpu.SMEM(mobility.shape, f32),
            pltpu.SMEM(stress.shape, f32),
            pltpu.VMEM(translation.shape, f32),
            pltpu.SemaphoreType.DMA((7,)),
            pltpu.VMEM((4, 4, 4, 16, slots), f32),
            pltpu.VMEM((2, sizes[2], 8, slots), f32),
            pltpu.VMEM((sizes[0], chips, 8, slots), f32),
            pltpu.VMEM((sizes[0], chips, 8, slots), f32),
            pltpu.VMEM((16 * source_rows, slots), f32),
            pltpu.VMEM((16 * split_rows, slots), f32),
            pltpu.VMEM((8 * term_rows, slots), f32),
            pltpu.VMEM((8, 2 * source_rows, 2 * slots), bf16),
            pltpu.VMEM((2, slots, 4 * split_rows), bf16),
            pltpu.VMEM((64, 2 * source_rows, 2 * slots), bf16),
            pltpu.VMEM((16, slots, 4 * split_rows), bf16),
            pltpu.VMEM((8, 4, 4 * split_rows, 2 * slots), bf16),
            pltpu.VMEM((8, slots, slots), bf16),
            pltpu.VMEM((slots, 6 * slots), bf16),
            pltpu.VMEM((sizes[0] * chips * 8, 4 * sizes[2] * 8), bf16),
            pltpu.VMEM((8 * source_rows, slots), f32),
            pltpu.VMEM((8 * source_rows, slots), f32),
            pltpu.VMEM((8 * source_rows, slots), f32),
            pltpu.VMEM((8 * source_rows, slots), f32),
            pltpu.SemaphoreType.DMA((26,)),
            pltpu.SemaphoreType.DMA((26,)),
            pltpu.SemaphoreType.DMA((2, sizes[2])),
            pltpu.SemaphoreType.DMA((2, sizes[2])),
            pltpu.SemaphoreType.DMA((sizes[0], chips)),
            pltpu.SemaphoreType.DMA((sizes[0], chips)),
        ],
        compiler_params=pltpu.CompilerParams(
            collective_id=0, has_side_effects=True, vmem_limit_bytes=60 * 1024 * 1024
        ),
    )(
        offsets.reshape(flat),
        lines.reshape(flat),
        burgers.reshape(flat),
        counts,
        mobility,
        stress,
        translation,
    )
    return result.reshape(shape)


def solution(mesh):
    sizes = tuple(mesh.shape[name] for name in ("gx", "gy", "gz"))
    placed = (
        P(None, "gx", "gy", "gz", None),
        P(None, "gx", "gy", "gz", None),
        P(None, "gx", "gy", "gz", None),
        P("gx", "gy", "gz"),
        P("gx", "gy", "gz"),
        P(),
        P(),
    )
    return jax.shard_map(
        functools.partial(body, sizes),
        mesh=mesh,
        in_specs=placed,
        out_specs=P(None, "gx", "gy", "gz", None),
        check_vma=False,
    )
```

```python
import functools

import jax
import jax.numpy as jnp
from jax import lax
from jax.experimental import pallas as pl
from jax.experimental.pallas import tpu as pltpu
from jax.sharding import PartitionSpec as P

MESH = pl.DeviceIdType.MESH
core_square = 0.0625
near_scale = 0.01
slots = 128
terms = 35
term_rows = 40
source_rows = 40
split_rows = 32
f32, bf16 = jnp.float32, jnp.bfloat16

offsets_26 = [
    (x, y, z)
    for x in (-1, 0, 1)
    for y in (-1, 0, 1)
    for z in (-1, 0, 1)
    if (x, y, z) != (0, 0, 0)
]


def exponent_list():
    result = []
    for first in range(5):
        for second in range(5 - first):
            for third in range(5 - first - second):
                result.append((first, second, third))
    return result


def crossed(left, right):
    return [
        left[1] * right[2] - left[2] * right[1],
        left[2] * right[0] - left[0] * right[2],
        left[0] * right[1] - left[1] * right[0],
    ]


def high_low(value):
    high = value.astype(bf16).astype(f32)
    return high, value - high


def split_three(value):
    first, rest = high_low(value)
    second, rest = high_low(rest)
    return [first, second, rest.astype(bf16).astype(f32)]


def two_parts(value):
    high = value.astype(bf16)
    return high, (value - high.astype(f32)).astype(bf16)


def source_values(position, line, charge):
    pairs = [charge[a] * line[b] for a in range(3) for b in range(3)]
    projection = sum(charge[c] * position[c] for c in range(3))
    rows = list(pairs)
    for c in range(3):
        rows += [position[c] * value for value in pairs]
    rows += [projection * line[c] for c in range(3)]
    rows.append(jnp.zeros_like(projection))
    splits = []
    for c in range(3):
        first, second, third = split_three(position[c])
        splits += [first, first, first, second, second, third]
    splits += split_three(sum(position[c] * position[c] for c in range(3)))
    one = jnp.ones_like(projection)
    zero = jnp.zeros_like(projection)
    splits += [one] * 3 + [zero] * 8
    return rows, splits


def target_values(position, charge):
    squares = sum(position[c] * position[c] for c in range(3)) + core_square
    projection = sum(charge[c] * position[c] for c in range(3))
    zero = jnp.zeros_like(squares)
    one = jnp.ones_like(squares)
    distance, along = [], []
    for c in range(3):
        first, second, third = split_three(-2.0 * position[c])
        distance += [first, second, third, first, second, first]
        first, second, third = split_three(charge[c])
        along += [first, second, third, first, second, first]
    distance += [one] * 3 + split_three(squares) + [zero] * 8
    along += [zero] * 3 + split_three(-projection) + [zero] * 8
    return distance, along


def store_rows(ref, values, stride, first=0):
    for n, value in enumerate(values):
        ref[pl.ds(first + n, 8, stride=stride), :] = value


def eight_cells(halo, group, n):
    flat = halo.reshape(64 * 16, slots)
    return flat[pl.ds(group * 8 * 16 + n, 8, stride=16), :]


def pack_sources(stage_rows, stage_split, out_rows, out_split, first, first_split, part=0):
    zero = jnp.zeros((source_rows, slots), f32)
    for cell in range(8):
        value = stage_rows[pl.ds((8 * part + cell) * source_rows, source_rows), :]
        high, low = high_low(value)
        out_rows[first + cell, :, pl.ds(0, slots)] = jnp.concatenate([high, low], 0).astype(bf16)
        out_rows[first + cell, :, pl.ds(slots, slots)] = jnp.concatenate([high, zero], 0).astype(
            bf16
        )
    for half in range(2):
        value = stage_split[pl.ds((2 * part + half) * 4 * split_rows, 4 * split_rows), :]
        out_split[first_split + half] = value.T.astype(bf16)


def products(groups, transpose=False):
    def scope(*totals):
        turn = [0, 0]
        for n, pairs in enumerate(groups):
            for left, right in pairs:
                staged = turn[n % 2] % 2
                turn[n % 2] += 1
                pltpu.matmul_push_rhs(right, staged, n % 2, transpose=transpose)
                pltpu.matmul_acc_lhs(totals[n], left, load_staged_rhs=staged)
        return [pltpu.matmul_pop(total) for total in totals]

    accumulators = [
        pltpu.ACC(n % 2)((pairs[0][0].shape[0], 2 * slots), f32) for n, pairs in enumerate(groups)
    ]
    return pl.run_scoped(scope, *accumulators)


chunk = 32
chunks = slots // chunk
ahead = 3


def near_sums(blocks, plan, target_rows, store, begin=0, end=8):
    count = len(blocks)
    held = ahead + 1

    def scope(total, *buffers):
        def buffer(p, n):
            return buffers[p % held * chunks + n]

        def stage(p, k):
            block = plan(k, p)[0]
            rhs = jnp.concatenate([target_rows[k, block], jnp.zeros((slots, 2 * slots), bf16)], 0)
            pltpu.matmul_push_rhs(rhs, 0, 0)

        firsts = [p for p in range(count) if p == 0 or blocks[p] != blocks[p - 1]]

        def start(p, k, after):
            _, splits, index, _, _ = plan(k, p)
            for n in range(chunks):
                left = splits[index, pl.ds(n * chunk, chunk), :]
                left = jnp.concatenate([left, jnp.zeros((chunk, slots), bf16)], 1)
                load = 0 if p in firsts and n == 0 else None
                pltpu.matmul_acc_lhs(buffer(p, n), left, load_staged_rhs=load)
            if p in firsts:
                later = firsts.index(p) + 1
                if later < len(firsts):
                    stage(firsts[later], k)
                else:
                    stage(0, after)

        def finish(p, k):
            highs, lows = [], []
            for n in range(chunks):
                both = pltpu.matmul_pop(buffer(p, n))
                inverse = lax.rsqrt(both[:, :slots])
                square = inverse * inverse
                cube = square * inverse
                value = jnp.concatenate([cube, cube * square * both[:, slots:]], 1)
                high, low = two_parts(value)
                highs.append(high)
                lows.append(low)
            if p == 0:
                store(jnp.maximum(k - 1, begin), pltpu.matmul_pop(total))
            _, _, _, rows, place = plan(k, p)
            pltpu.matmul_push_rhs(jnp.concatenate(highs + lows, 0), p % 2, 1)
            pltpu.matmul_acc_lhs(total, rows[place], load_staged_rhs=p % 2)

        def target(k, _):
            after = jnp.minimum(k + 1, end - 1)
            for p in range(count):
                finish(p, k)
                if p + ahead < count:
                    start(p + ahead, k, after)
                else:
                    start(p + ahead - count, after, after)
            return 0

        stage(0, begin)
        for p in range(ahead):
            start(p, begin, begin)
        lax.fori_loop(begin, end, target, 0)
        store(end - 1, pltpu.matmul_pop(total))
        pltpu.matmul_acc_lhs(
            buffer(0, 0), jnp.zeros((chunk, 2 * slots), bf16), load_staged_rhs=0
        )
        for p in range(ahead):
            for n in range(chunks):
                pltpu.matmul_pop(buffer(p, n))

    pl.run_scoped(
        scope,
        pltpu.ACC(1)((2 * source_rows, 2 * slots), f32),
        *[pltpu.ACC(0)((chunk, 2 * slots), f32)] * (held * chunks),
    )


def kernel(
    sizes,
    offsets_in,
    lines_in,
    burgers_in,
    counts_in,
    mobility_in,
    stress_in,
    translation_in,
    out_ref,
    offsets_ref,
    lines_ref,
    burgers_ref,
    counts_ref,
    mobility_ref,
    stress_ref,
    translation_ref,
    operand_sem,
    halo,
    gathered,
    partial,
    received,
    stage_rows,
    stage_split,
    stage_poly,
    local_rows,
    local_split,
    halo_rows,
    halo_split,
    target_rows,
    poly_rows,
    translation_rows,
    weight_rows,
    near_w,
    near_c,
    halo_w,
    halo_c,
    halo_send,
    halo_recv,
    gather_send,
    gather_recv,
    reduce_send,
    reduce_recv,
):
    operands = [
        (counts_in, counts_ref),
        (offsets_in, offsets_ref),
        (lines_in, lines_ref),
        (burgers_in, burgers_ref),
        (mobility_in, mobility_ref),
        (stress_in, stress_ref),
        (translation_in, translation_ref),
    ]
    loads = [
        pltpu.make_async_copy(source, target, operand_sem.at[n])
        for n, (source, target) in enumerate(operands)
    ]
    for load in loads:
        load.start()

    me = [lax.axis_index(name) for name in ("gx", "gy", "gz")]
    count_x, count_y, count_z = sizes

    def device(step_x, step_y, step_z):
        return tuple(
            lax.rem(me[axis] + step + sizes[axis], sizes[axis])
            for axis, step in enumerate((step_x, step_y, step_z))
        )

    chips = count_y // 2
    core = lax.rem(me[1], 2)
    over = 1 - 2 * core
    sources = [(r, b) for r in range(2) for b in range(count_z) if (r, b) != (0, 0)]
    goals = [(u, v) for u in range(count_x) for v in range(chips) if (u, v) != (0, 0)]
    partners = list(offsets_26)
    partners += [(0, r * over, b) for r, b in sources if b not in (0, 1, count_z - 1)]
    partners += [(u, 2 * v, 0) for u, v in goals if v or u not in (1, count_x - 1)]
    barrier = pltpu.get_barrier_semaphore()
    for step in partners:
        pl.semaphore_signal(barrier, inc=1, device_id=device(*step), device_id_type=MESH)

    shape = (count_x * chips * 8, 2 * count_z * 8)
    goal = lax.broadcasted_iota(jnp.int32, shape, 0)
    source = lax.broadcasted_iota(jnp.int32, shape, 1)
    apart = [
        2 * (goal // (8 * chips)) + goal // 4 % 2 - source // 4 % 2,
        4 * (goal // 8 % chips) - 2 * over * (source // (8 * count_z)) + goal // 2 % 2 - source // 2 % 2,
        2 * (source // 8 % count_z) + goal % 2 - source % 2,
    ]
    largest, total_sq = 0, 0
    for axis in range(3):
        extent = 2 * sizes[axis]
        steps = lax.rem(apart[axis] + extent, extent)
        steps = jnp.minimum(steps, extent - steps)
        largest = jnp.maximum(largest, steps)
        total_sq = total_sq + steps * steps
    weights = jnp.where(largest > 1, lax.rsqrt(jnp.maximum(total_sq, 1).astype(f32)), 0.0)
    weight_rows[...] = jnp.concatenate(two_parts(weights), 1)

    target_rows[...] = jnp.zeros(target_rows.shape, bf16)

    for load in loads[:4]:
        load.wait()
    cell = lax.broadcasted_iota(jnp.int32, (8, slots), 0)
    lane = lax.broadcasted_iota(jnp.int32, (8, slots), 1)
    counts = jnp.zeros((8, slots), jnp.int32)
    for k in range(8):
        where = (k // 4, k // 2 % 2, k % 2)
        counts = jnp.where(cell == k, counts_ref[where], counts)
    mask = jnp.where(lane < counts, 1.0, 0.0).astype(f32)
    offsets = [offsets_ref[c] for c in range(3)]
    lines = [lines_ref[c] for c in range(3)]
    charge = [burgers_ref[c] * mask for c in range(3)]

    powers = []
    for base in offsets:
        square = base * base
        powers.append([jnp.ones_like(base), base, square, square * base, square * square])
    poly = []
    for first, second, third in exponent_list():
        factors = [powers[c][e] for c, e in enumerate((first, second, third)) if e]
        value = factors[0] if factors else powers[0][0]
        for factor in factors[1:]:
            value = value * factor
        poly.append(value)
    poly += [jnp.zeros((8, slots), f32)] * (term_rows - terms)
    store_rows(stage_poly, poly, term_rows)
    pad = jnp.zeros((slots - 2 * term_rows, slots), f32)
    for k in range(8):
        high, low = high_low(stage_poly[pl.ds(k * term_rows, term_rows), :])
        poly_rows[k] = jnp.concatenate([high, low, pad], 0).astype(bf16)
    dipole = crossed(charge, lines)
    highs, lows = [], []
    for value in dipole:
        high, low = high_low(value)
        highs.append(high)
        lows.append(low)
    zero = jnp.zeros((8, slots), f32)
    pairs = []
    for first in range(0, 8, 2):
        left = []
        for k in (first, first + 1):
            rows = [jnp.where(cell == k, part, 0.0) for part in highs] + [zero]
            rows += [jnp.where(cell == k, part, 0.0) for part in lows] + [zero]
            left.append(jnp.concatenate(rows, 0).astype(bf16))
        right = jnp.concatenate([poly_rows[first], poly_rows[first + 1]], 1)
        right = jnp.concatenate([right, jnp.zeros((slots, 2 * slots), bf16)], 0)
        pairs.append((jnp.concatenate(left, 1), right))
    moments = sum(products([pairs[:2], pairs[2:]], transpose=True))[:, :slots]
    moments = moments[:32] + moments[32:]
    total = zero
    for m in range(3):
        part = moments[8 * m : 8 * m + 8]
        part = part + pltpu.roll(part, slots - term_rows, 1)
        part = jnp.where(lane < terms, part, 0.0)
        total = total + (part if m == 0 else pltpu.roll(part, terms * m, 1))
    gathered[0, 0] = total * (1.0 / slots)

    for c in range(3):
        for first, value in ((0, offsets), (3, lines), (6, charge)):
            for k in range(8):
                where = (1 + k // 4, 1 + k // 2 % 2, 1 + k % 2, pl.ds(first + c, 1))
                halo[where] = value[c][k : k + 1]

    pl.semaphore_wait(barrier, len(partners))

    copies_in = [
        pltpu.make_async_remote_copy(
            src_ref=gathered.at[0, 0],
            dst_ref=gathered.at[r, b],
            send_sem=gather_send.at[r, b],
            recv_sem=gather_recv.at[r, b],
            device_id=device(0, r * over, b),
            device_id_type=MESH,
        )
        for r, b in sources
    ]
    for copy in copies_in:
        copy.start()
    sides = {
        -1: (pl.ds(1, 1), pl.ds(3, 1)),
        0: (pl.ds(1, 2), pl.ds(1, 2)),
        1: (pl.ds(2, 1), pl.ds(0, 1)),
    }
    copies_halo = []
    for n, step in enumerate(offsets_26):
        source = tuple(sides[s][0] for s in step) + (pl.ds(0, 9),)
        target = tuple(sides[s][1] for s in step) + (pl.ds(0, 9),)
        copies_halo.append(
            pltpu.make_async_remote_copy(
                src_ref=halo.at[source],
                dst_ref=halo.at[target],
                send_sem=halo_send.at[n],
                recv_sem=halo_recv.at[n],
                device_id=device(*step),
                device_id_type=MESH,
            )
        )
    for copy in copies_halo:
        copy.start()

    corner = [cell // 4, cell // 2 % 2, cell % 2]
    position = [offsets[c] + (corner[c].astype(f32) - 0.5) for c in range(3)]
    rows, splits = source_values(position, lines, charge)
    store_rows(stage_rows, rows, source_rows)
    store_rows(stage_split, splits, split_rows)
    pack_sources(stage_rows, stage_split, local_rows, local_split, 0, 0)
    distance, along = target_values(position, charge)
    for side, values in enumerate((distance, along)):
        store_rows(stage_split, values, split_rows)
        for k in range(8):
            value = stage_split[pl.ds(k * split_rows, split_rows), :].astype(bf16)
            for block in range(4):
                target_rows[
                    k, block, pl.ds(block * split_rows, split_rows), pl.ds(side * slots, slots)
                ] = value

    local_order = [4 * half + place for place in range(4) for half in range(2)]

    def local_plan(k, p):
        source = local_order[p]
        return source % 4, local_split, source // 4, local_rows, source

    def keep(ref_w, ref_c, k, value):
        value = value[:source_rows] + value[source_rows:]
        where = pl.ds(pl.multiple_of(k * source_rows, 8), source_rows)
        ref_w[where, :] = value[:, :slots]
        ref_c[where, :] = value[:, slots:]

    halo_order = [(n, z) for z in range(3) for n in range(9) if z == 2 or n in (2, 5, 6, 7, 8)]

    def halo_plan(k, p):
        n, z = halo_order[p]
        x = (1, 2, 3 * (k // 4))[n // 3]
        y = (1, 2, 3 * (k // 2 % 2))[n % 3]
        z = (1, 2, 3 * (k % 2))[z]
        return z, halo_split, 4 * x + y, halo_rows, 16 * x + 4 * y + z

    def near_local(begin, end):
        blocks = [source % 4 for source in local_order]
        keep_local = functools.partial(keep, near_w, near_c)
        near_sums(blocks, local_plan, target_rows, keep_local, begin, end)

    def near_halo():
        blocks = [z for _, z in halo_order]
        near_sums(blocks, halo_plan, target_rows, functools.partial(keep, halo_w, halo_c))

    near_local(0, 8)
    for load in loads[4:]:
        load.wait()
    mobility = jnp.zeros((8, slots), f32)
    for k in range(8):
        where = (k // 4, k // 2 % 2, k % 2)
        mobility = jnp.where(cell == k, mobility_ref[where], mobility)
    translation = translation_ref[...]
    for m in range(3):
        value = translation if m == 0 else pltpu.roll(translation, slots - terms * m, 1)
        value = jnp.where(lax.broadcasted_iota(jnp.int32, (slots, slots), 1) < terms, value, 0.0)
        high, low = two_parts(value)
        translation_rows[:, pl.ds(2 * m * slots, slots)] = high
        translation_rows[:, pl.ds((2 * m + 1) * slots, slots)] = low


    for copy in copies_in:
        copy.wait()
    high, low = two_parts(gathered[...].reshape(2 * count_z * 8, slots))
    both = jnp.concatenate([high, low], 1)
    both = jnp.concatenate([both, both], 0)
    half = weight_rows.shape[0] // 2
    values = products([[(weight_rows[pl.ds(n * half, half), :], both)] for n in range(2)])
    value = jnp.concatenate(values, 0)
    value = value[:, :slots] + value[:, slots:]
    partial[...] = value.reshape(count_x, chips, 8, slots)
    copies_out = [
        pltpu.make_async_remote_copy(
            src_ref=partial.at[u, v],
            dst_ref=received.at[u, v],
            send_sem=reduce_send.at[u, v],
            recv_sem=reduce_recv.at[u, v],
            device_id=device(u, 2 * v, 0),
            device_id_type=MESH,
        )
        for u, v in goals
    ]
    for copy in copies_out:
        copy.start()

    for copy in copies_halo:
        copy.wait()

    def prepare(planes, _):
        for part in range(4):
            group = 4 * planes + part
            value = [eight_cells(halo, group, n) for n in range(9)]
            place = [
                jnp.zeros((8, slots), jnp.int32) + 2 * planes + part // 2,
                part % 2 * 2 + cell // 4,
                cell % 4,
            ]
            position = [value[c] + (place[c].astype(f32) - 1.5) for c in range(3)]
            rows, splits = source_values(position, value[3:6], value[6:9])
            store_rows(stage_rows, rows, source_rows, 8 * source_rows * part)
            store_rows(stage_split, splits, split_rows, 8 * split_rows * part)
        for part in range(4):
            group = 4 * planes + part
            pack_sources(
                stage_rows, stage_split, halo_rows, halo_split, group * 8, group * 2, part
            )
        return 0

    lax.fori_loop(0, 2, prepare, 0)
    near_halo()

    def row(refs, n):
        return sum(ref[pl.ds(n, 8, stride=source_rows), :] for ref in refs)

    near_w, near_c = (near_w, halo_w), (near_c, halo_c)

    pairs = [charge[a] * lines[b] for a in range(3) for b in range(3)]
    still = sum(pairs[n] * row(near_w, n) for n in range(9))
    near = []
    for c in range(3):
        first = sum(pairs[n] * row(near_w, 9 + 9 * c + n) for n in range(9))
        second = row(near_c, 36 + c) - sum(position[b] * row(near_c, 3 * b + c) for b in range(3))
        near.append(near_scale * (first - position[c] * still + second))

    stressed = [sum(stress_ref[a, b] * charge[b] for b in range(3)) for a in range(3)]
    applied = crossed(stressed, lines)
    known = [near[c] + applied[c] for c in range(3)]
    shorten = 1.0 / jnp.maximum(sum(lines[c] * lines[c] for c in range(3)), 1.0)
    scale = mobility * mask

    for copy in copies_out:
        copy.wait()
    received[0, 0] = partial[0, 0]
    summed_moments = jnp.sum(received[...].reshape(count_x * chips, 8, slots), 0)
    high, low = high_low(summed_moments)
    left = jnp.concatenate([high, low], 0).astype(bf16)
    left = jnp.concatenate([left, jnp.zeros((16, slots), bf16)], 1)
    groups = []
    for m in range(3):
        right = translation_rows[:, pl.ds(2 * m * slots, 2 * slots)]
        groups.append([(left, jnp.concatenate([right, jnp.zeros((slots, 2 * slots), bf16)], 0))])
    highs, lows = [], []
    for value in products(groups):
        value = value[:8] + value[8:]
        value = value[:, :slots] + value[:, slots:]
        for part, result in zip(high_low(value), (highs, lows)):
            result.append(part + pltpu.roll(part, term_rows, 1))
    left = [jnp.concatenate(parts + [zero], 0).astype(bf16) for parts in (highs, lows)]
    left = jnp.concatenate(left, 1)
    groups = []
    for first in range(0, 8, 2):
        right = jnp.concatenate([poly_rows[first], poly_rows[first + 1]], 1)
        groups.append([(left, jnp.concatenate([right, right], 0))])
    far = [zero] * 3
    for pair, fields in enumerate(products(groups)):
        for m in range(3):
            for n in range(2):
                field = fields[8 * m : 8 * m + 8, n * slots : (n + 1) * slots]
                far[m] = jnp.where(cell == 2 * pair + n, field, far[m])
    far = [value * mask for value in far]

    force = [known[c] + far[c] for c in range(3)]
    along = sum(force[c] * lines[c] for c in range(3))
    along = along * shorten
    for c in range(3):
        out_ref[c] = scale * (force[c] - along * lines[c])


def body(sizes, offsets, lines, burgers, counts, mobility, stress, translation):
    vmem, hbm = (pl.BlockSpec(memory_space=space) for space in (pltpu.VMEM, pltpu.HBM))
    shape = offsets.shape
    flat = (3, 8, slots)
    chips = sizes[1] // 2
    result = pl.pallas_call(
        functools.partial(kernel, sizes),
        out_shape=pltpu.VMEM(flat, f32),
        in_specs=[hbm] * 7,
        out_specs=vmem,
        scratch_shapes=[
            pltpu.VMEM(flat, f32),
            pltpu.VMEM(flat, f32),
            pltpu.VMEM(flat, f32),
            pltpu.SMEM(counts.shape, jnp.int32),
            pltpu.SMEM(mobility.shape, f32),
            pltpu.SMEM(stress.shape, f32),
            pltpu.VMEM(translation.shape, f32),
            pltpu.SemaphoreType.DMA((7,)),
            pltpu.VMEM((4, 4, 4, 16, slots), f32),
            pltpu.VMEM((2, sizes[2], 8, slots), f32),
            pltpu.VMEM((sizes[0], chips, 8, slots), f32),
            pltpu.VMEM((sizes[0], chips, 8, slots), f32),
            pltpu.VMEM((32 * source_rows, slots), f32),
            pltpu.VMEM((32 * split_rows, slots), f32),
            pltpu.VMEM((8 * term_rows, slots), f32),
            pltpu.VMEM((8, 2 * source_rows, 2 * slots), bf16),
            pltpu.VMEM((2, slots, 4 * split_rows), bf16),
            pltpu.VMEM((64, 2 * source_rows, 2 * slots), bf16),
            pltpu.VMEM((16, slots, 4 * split_rows), bf16),
            pltpu.VMEM((8, 4, 4 * split_rows, 2 * slots), bf16),
            pltpu.VMEM((8, slots, slots), bf16),
            pltpu.VMEM((slots, 6 * slots), bf16),
            pltpu.VMEM((sizes[0] * chips * 8, 4 * sizes[2] * 8), bf16),
            pltpu.VMEM((8 * source_rows, slots), f32),
            pltpu.VMEM((8 * source_rows, slots), f32),
            pltpu.VMEM((8 * source_rows, slots), f32),
            pltpu.VMEM((8 * source_rows, slots), f32),
            pltpu.SemaphoreType.DMA((26,)),
            pltpu.SemaphoreType.DMA((26,)),
            pltpu.SemaphoreType.DMA((2, sizes[2])),
            pltpu.SemaphoreType.DMA((2, sizes[2])),
            pltpu.SemaphoreType.DMA((sizes[0], chips)),
            pltpu.SemaphoreType.DMA((sizes[0], chips)),
        ],
        compiler_params=pltpu.CompilerParams(
            collective_id=0, has_side_effects=True, vmem_limit_bytes=60 * 1024 * 1024
        ),
    )(
        offsets.reshape(flat),
        lines.reshape(flat),
        burgers.reshape(flat),
        counts,
        mobility,
        stress,
        translation,
    )
    return result.reshape(shape)


def solution(mesh):
    sizes = tuple(mesh.shape[name] for name in ("gx", "gy", "gz"))
    placed = (
        P(None, "gx", "gy", "gz", None),
        P(None, "gx", "gy", "gz", None),
        P(None, "gx", "gy", "gz", None),
        P("gx", "gy", "gz"),
        P("gx", "gy", "gz"),
        P(),
        P(),
    )
    return jax.shard_map(
        functools.partial(body, sizes),
        mesh=mesh,
        in_specs=placed,
        out_specs=P(None, "gx", "gy", "gz", None),
        check_vma=False,
    )
```

```python
import functools

import jax
import jax.numpy as jnp
from jax import lax
from jax.experimental import pallas as pl
from jax.experimental.pallas import tpu as pltpu
from jax.sharding import PartitionSpec as P

MESH = pl.DeviceIdType.MESH
core_square = 0.0625
near_scale = 0.01
slots = 128
terms = 35
term_rows = 40
source_rows = 40
split_rows = 32
f32, bf16 = jnp.float32, jnp.bfloat16

offsets_26 = [
    (x, y, z)
    for x in (-1, 0, 1)
    for y in (-1, 0, 1)
    for z in (-1, 0, 1)
    if (x, y, z) != (0, 0, 0)
]


def exponent_list():
    result = []
    for first in range(5):
        for second in range(5 - first):
            for third in range(5 - first - second):
                result.append((first, second, third))
    return result


def crossed(left, right):
    return [
        left[1] * right[2] - left[2] * right[1],
        left[2] * right[0] - left[0] * right[2],
        left[0] * right[1] - left[1] * right[0],
    ]


def high_low(value):
    high = value.astype(bf16).astype(f32)
    return high, value - high


def split_three(value):
    first, rest = high_low(value)
    second, rest = high_low(rest)
    return [first, second, rest.astype(bf16).astype(f32)]


def two_parts(value):
    high = value.astype(bf16)
    return high, (value - high.astype(f32)).astype(bf16)


def source_values(position, line, charge):
    pairs = [charge[a] * line[b] for a in range(3) for b in range(3)]
    projection = sum(charge[c] * position[c] for c in range(3))
    rows = list(pairs)
    for c in range(3):
        rows += [position[c] * value for value in pairs]
    rows += [projection * line[c] for c in range(3)]
    rows.append(jnp.zeros_like(projection))
    splits = []
    for c in range(3):
        first, second, third = split_three(position[c])
        splits += [first, first, first, second, second, third]
    splits += split_three(sum(position[c] * position[c] for c in range(3)))
    one = jnp.ones_like(projection)
    zero = jnp.zeros_like(projection)
    splits += [one] * 3 + [zero] * 8
    return rows, splits


def target_values(position, charge):
    squares = sum(position[c] * position[c] for c in range(3)) + core_square
    projection = sum(charge[c] * position[c] for c in range(3))
    zero = jnp.zeros_like(squares)
    one = jnp.ones_like(squares)
    distance, along = [], []
    for c in range(3):
        first, second, third = split_three(-2.0 * position[c])
        distance += [first, second, third, first, second, first]
        first, second, third = split_three(charge[c])
        along += [first, second, third, first, second, first]
    distance += [one] * 3 + split_three(squares) + [zero] * 8
    along += [zero] * 3 + split_three(-projection) + [zero] * 8
    return distance, along


def store_rows(ref, values, stride, first=0):
    for n, value in enumerate(values):
        ref[pl.ds(first + n, 8, stride=stride), :] = value


def eight_cells(halo, group, n):
    flat = halo.reshape(64 * 16, slots)
    return flat[pl.ds(group * 8 * 16 + n, 8, stride=16), :]


def pack_sources(stage_rows, stage_split, out_rows, out_split, first, first_split, part=0):
    zero = jnp.zeros((source_rows, slots), f32)
    for cell in range(8):
        value = stage_rows[pl.ds((8 * part + cell) * source_rows, source_rows), :]
        high, low = high_low(value)
        out_rows[first + cell, :, pl.ds(0, slots)] = jnp.concatenate([high, low], 0).astype(bf16)
        out_rows[first + cell, :, pl.ds(slots, slots)] = jnp.concatenate([high, zero], 0).astype(
            bf16
        )
    for half in range(2):
        value = stage_split[pl.ds((2 * part + half) * 4 * split_rows, 4 * split_rows), :]
        out_split[first_split + half] = value.T.astype(bf16)


def products(groups, transpose=False):
    def scope(*totals):
        turn = [0, 0]
        for n, pairs in enumerate(groups):
            for left, right in pairs:
                staged = turn[n % 2] % 2
                turn[n % 2] += 1
                pltpu.matmul_push_rhs(right, staged, n % 2, transpose=transpose)
                pltpu.matmul_acc_lhs(totals[n], left, load_staged_rhs=staged)
        return [pltpu.matmul_pop(total) for total in totals]

    accumulators = [
        pltpu.ACC(n % 2)((pairs[0][0].shape[0], 2 * slots), f32) for n, pairs in enumerate(groups)
    ]
    return pl.run_scoped(scope, *accumulators)


chunk = 32
chunks = slots // chunk
ahead = 3


def near_sums(blocks, plan, target_rows, store, begin=0, end=8):
    count = len(blocks)
    held = ahead + 1

    def scope(total, *buffers):
        def buffer(p, n):
            return buffers[p % held * chunks + n]

        def stage(p, k):
            block = plan(k, p)[0]
            rhs = jnp.concatenate([target_rows[k, block], jnp.zeros((slots, 2 * slots), bf16)], 0)
            pltpu.matmul_push_rhs(rhs, 0, 0)

        firsts = [p for p in range(count) if p == 0 or blocks[p] != blocks[p - 1]]

        def start(p, k, after):
            _, splits, index, _, _ = plan(k, p)
            for n in range(chunks):
                left = splits[index, pl.ds(n * chunk, chunk), :]
                left = jnp.concatenate([left, jnp.zeros((chunk, slots), bf16)], 1)
                load = 0 if p in firsts and n == 0 else None
                pltpu.matmul_acc_lhs(buffer(p, n), left, load_staged_rhs=load)
            if p in firsts:
                later = firsts.index(p) + 1
                if later < len(firsts):
                    stage(firsts[later], k)
                else:
                    stage(0, after)

        def finish(p, k):
            highs, lows = [], []
            for n in range(chunks):
                both = pltpu.matmul_pop(buffer(p, n))
                inverse = lax.rsqrt(both[:, :slots])
                square = inverse * inverse
                cube = square * inverse
                value = jnp.concatenate([cube, cube * square * both[:, slots:]], 1)
                high, low = two_parts(value)
                highs.append(high)
                lows.append(low)
            if p == 0:
                store(jnp.maximum(k - 1, begin), pltpu.matmul_pop(total))
            _, _, _, rows, place = plan(k, p)
            pltpu.matmul_push_rhs(jnp.concatenate(highs + lows, 0), p % 2, 1)
            pltpu.matmul_acc_lhs(total, rows[place], load_staged_rhs=p % 2)

        def target(k, _):
            after = jnp.minimum(k + 1, end - 1)
            for p in range(count):
                finish(p, k)
                if p + ahead < count:
                    start(p + ahead, k, after)
                else:
                    start(p + ahead - count, after, after)
            return 0

        stage(0, begin)
        for p in range(ahead):
            start(p, begin, begin)
        lax.fori_loop(begin, end, target, 0)
        store(end - 1, pltpu.matmul_pop(total))
        pltpu.matmul_acc_lhs(
            buffer(0, 0), jnp.zeros((chunk, 2 * slots), bf16), load_staged_rhs=0
        )
        for p in range(ahead):
            for n in range(chunks):
                pltpu.matmul_pop(buffer(p, n))

    pl.run_scoped(
        scope,
        pltpu.ACC(1)((2 * source_rows, 2 * slots), f32),
        *[pltpu.ACC(0)((chunk, 2 * slots), f32)] * (held * chunks),
    )


def kernel(
    sizes,
    offsets_in,
    lines_in,
    burgers_in,
    counts_in,
    mobility_in,
    stress_in,
    translation_in,
    out_ref,
    offsets_ref,
    lines_ref,
    burgers_ref,
    counts_ref,
    mobility_ref,
    stress_ref,
    translation_ref,
    operand_sem,
    halo,
    gathered,
    partial,
    received,
    stage_rows,
    stage_split,
    stage_poly,
    local_rows,
    local_split,
    halo_rows,
    halo_split,
    target_rows,
    poly_rows,
    translation_rows,
    weight_rows,
    near_w,
    near_c,
    halo_w,
    halo_c,
    halo_send,
    halo_recv,
    gather_send,
    gather_recv,
    reduce_send,
    reduce_recv,
):
    operands = [
        (counts_in, counts_ref),
        (offsets_in, offsets_ref),
        (lines_in, lines_ref),
        (burgers_in, burgers_ref),
        (mobility_in, mobility_ref),
        (stress_in, stress_ref),
        (translation_in, translation_ref),
    ]
    loads = [
        pltpu.make_async_copy(source, target, operand_sem.at[n])
        for n, (source, target) in enumerate(operands)
    ]
    for load in loads:
        load.start()

    me = [lax.axis_index(name) for name in ("gx", "gy", "gz")]
    count_x, count_y, count_z = sizes

    def device(step_x, step_y, step_z):
        return tuple(
            lax.rem(me[axis] + step + sizes[axis], sizes[axis])
            for axis, step in enumerate((step_x, step_y, step_z))
        )

    chips = count_y // 2
    core = lax.rem(me[1], 2)
    over = 1 - 2 * core
    sources = [(r, b) for r in range(2) for b in range(count_z) if (r, b) != (0, 0)]
    goals = [(u, v) for u in range(count_x) for v in range(chips) if (u, v) != (0, 0)]
    partners = list(offsets_26)
    partners += [(0, r * over, b) for r, b in sources if b not in (0, 1, count_z - 1)]
    partners += [(u, 2 * v, 0) for u, v in goals if v or u not in (1, count_x - 1)]
    barrier = pltpu.get_barrier_semaphore()
    for step in partners:
        pl.semaphore_signal(barrier, inc=1, device_id=device(*step), device_id_type=MESH)

    shape = (count_x * chips * 8, 2 * count_z * 8)
    goal = lax.broadcasted_iota(jnp.int32, shape, 0)
    source = lax.broadcasted_iota(jnp.int32, shape, 1)
    apart = [
        2 * (goal // (8 * chips)) + goal // 4 % 2 - source // 4 % 2,
        4 * (goal // 8 % chips) - 2 * over * (source // (8 * count_z)) + goal // 2 % 2 - source // 2 % 2,
        2 * (source // 8 % count_z) + goal % 2 - source % 2,
    ]
    largest, total_sq = 0, 0
    for axis in range(3):
        extent = 2 * sizes[axis]
        steps = lax.rem(apart[axis] + extent, extent)
        steps = jnp.minimum(steps, extent - steps)
        largest = jnp.maximum(largest, steps)
        total_sq = total_sq + steps * steps
    weights = jnp.where(largest > 1, lax.rsqrt(jnp.maximum(total_sq, 1).astype(f32)), 0.0)
    weight_rows[...] = jnp.concatenate(two_parts(weights), 1)

    target_rows[...] = jnp.zeros(target_rows.shape, bf16)

    for load in loads[:4]:
        load.wait()
    cell = lax.broadcasted_iota(jnp.int32, (8, slots), 0)
    lane = lax.broadcasted_iota(jnp.int32, (8, slots), 1)
    counts = jnp.zeros((8, slots), jnp.int32)
    for k in range(8):
        where = (k // 4, k // 2 % 2, k % 2)
        counts = jnp.where(cell == k, counts_ref[where], counts)
    mask = jnp.where(lane < counts, 1.0, 0.0).astype(f32)
    offsets = [offsets_ref[c] for c in range(3)]
    lines = [lines_ref[c] for c in range(3)]
    charge = [burgers_ref[c] * mask for c in range(3)]

    powers = []
    for base in offsets:
        square = base * base
        powers.append([jnp.ones_like(base), base, square, square * base, square * square])
    poly = []
    for first, second, third in exponent_list():
        factors = [powers[c][e] for c, e in enumerate((first, second, third)) if e]
        value = factors[0] if factors else powers[0][0]
        for factor in factors[1:]:
            value = value * factor
        poly.append(value)
    poly += [jnp.zeros((8, slots), f32)] * (term_rows - terms)
    store_rows(stage_poly, poly, term_rows)
    pad = jnp.zeros((slots - 2 * term_rows, slots), f32)
    for k in range(8):
        high, low = high_low(stage_poly[pl.ds(k * term_rows, term_rows), :])
        poly_rows[k] = jnp.concatenate([high, low, pad], 0).astype(bf16)
    dipole = crossed(charge, lines)
    highs, lows = [], []
    for value in dipole:
        high, low = high_low(value)
        highs.append(high)
        lows.append(low)
    zero = jnp.zeros((8, slots), f32)
    pairs = []
    for first in range(0, 8, 2):
        left = []
        for k in (first, first + 1):
            rows = [jnp.where(cell == k, part, 0.0) for part in highs] + [zero]
            rows += [jnp.where(cell == k, part, 0.0) for part in lows] + [zero]
            left.append(jnp.concatenate(rows, 0).astype(bf16))
        right = jnp.concatenate([poly_rows[first], poly_rows[first + 1]], 1)
        right = jnp.concatenate([right, jnp.zeros((slots, 2 * slots), bf16)], 0)
        pairs.append((jnp.concatenate(left, 1), right))
    moments = sum(products([pairs[:2], pairs[2:]], transpose=True))[:, :slots]
    moments = moments[:32] + moments[32:]
    total = zero
    for m in range(3):
        part = moments[8 * m : 8 * m + 8]
        part = part + pltpu.roll(part, slots - term_rows, 1)
        part = jnp.where(lane < terms, part, 0.0)
        total = total + (part if m == 0 else pltpu.roll(part, terms * m, 1))
    gathered[0, 0] = total * (1.0 / slots)

    pl.semaphore_wait(barrier, len(partners))

    copies_in = [
        pltpu.make_async_remote_copy(
            src_ref=gathered.at[0, 0],
            dst_ref=gathered.at[r, b],
            send_sem=gather_send.at[r, b],
            recv_sem=gather_recv.at[r, b],
            device_id=device(0, r * over, b),
            device_id_type=MESH,
        )
        for r, b in sources
    ]
    for copy in copies_in:
        copy.start()

    for c in range(3):
        for first, value in ((0, offsets), (3, lines), (6, charge)):
            for k in range(8):
                where = (1 + k // 4, 1 + k // 2 % 2, 1 + k % 2, pl.ds(first + c, 1))
                halo[where] = value[c][k : k + 1]

    sides = {
        -1: (pl.ds(1, 1), pl.ds(3, 1)),
        0: (pl.ds(1, 2), pl.ds(1, 2)),
        1: (pl.ds(2, 1), pl.ds(0, 1)),
    }
    copies_halo = []
    for n, step in enumerate(offsets_26):
        source = tuple(sides[s][0] for s in step) + (pl.ds(0, 9),)
        target = tuple(sides[s][1] for s in step) + (pl.ds(0, 9),)
        copies_halo.append(
            pltpu.make_async_remote_copy(
                src_ref=halo.at[source],
                dst_ref=halo.at[target],
                send_sem=halo_send.at[n],
                recv_sem=halo_recv.at[n],
                device_id=device(*step),
                device_id_type=MESH,
            )
        )
    for copy in copies_halo:
        copy.start()

    corner = [cell // 4, cell // 2 % 2, cell % 2]
    position = [offsets[c] + (corner[c].astype(f32) - 0.5) for c in range(3)]
    rows, splits = source_values(position, lines, charge)
    store_rows(stage_rows, rows, source_rows)
    store_rows(stage_split, splits, split_rows)
    pack_sources(stage_rows, stage_split, local_rows, local_split, 0, 0)
    distance, along = target_values(position, charge)
    for side, values in enumerate((distance, along)):
        store_rows(stage_split, values, split_rows)
        for k in range(8):
            value = stage_split[pl.ds(k * split_rows, split_rows), :].astype(bf16)
            for block in range(4):
                target_rows[
                    k, block, pl.ds(block * split_rows, split_rows), pl.ds(side * slots, slots)
                ] = value

    local_order = [4 * half + place for place in range(4) for half in range(2)]

    def local_plan(k, p):
        source = local_order[p]
        return source % 4, local_split, source // 4, local_rows, source

    def keep(ref_w, ref_c, k, value):
        value = value[:source_rows] + value[source_rows:]
        where = pl.ds(pl.multiple_of(k * source_rows, 8), source_rows)
        ref_w[where, :] = value[:, :slots]
        ref_c[where, :] = value[:, slots:]

    halo_order = [(n, z) for z in range(3) for n in range(9) if z == 2 or n in (2, 5, 6, 7, 8)]

    def halo_plan(k, p):
        n, z = halo_order[p]
        x = (1, 2, 3 * (k // 4))[n // 3]
        y = (1, 2, 3 * (k // 2 % 2))[n % 3]
        z = (1, 2, 3 * (k % 2))[z]
        return z, halo_split, 4 * x + y, halo_rows, 16 * x + 4 * y + z

    def near_local(begin, end):
        blocks = [source % 4 for source in local_order]
        keep_local = functools.partial(keep, near_w, near_c)
        near_sums(blocks, local_plan, target_rows, keep_local, begin, end)

    def near_halo():
        blocks = [z for _, z in halo_order]
        near_sums(blocks, halo_plan, target_rows, functools.partial(keep, halo_w, halo_c))

    near_local(0, 8)
    for load in loads[4:]:
        load.wait()
    mobility = jnp.zeros((8, slots), f32)
    for k in range(8):
        where = (k // 4, k // 2 % 2, k % 2)
        mobility = jnp.where(cell == k, mobility_ref[where], mobility)
    translation = translation_ref[...]
    for m in range(3):
        value = translation if m == 0 else pltpu.roll(translation, slots - terms * m, 1)
        value = jnp.where(lax.broadcasted_iota(jnp.int32, (slots, slots), 1) < terms, value, 0.0)
        high, low = two_parts(value)
        translation_rows[:, pl.ds(2 * m * slots, slots)] = high
        translation_rows[:, pl.ds((2 * m + 1) * slots, slots)] = low


    for copy in copies_in:
        copy.wait()
    high, low = two_parts(gathered[...].reshape(2 * count_z * 8, slots))
    both = jnp.concatenate([high, low], 1)
    both = jnp.concatenate([both, both], 0)
    half = weight_rows.shape[0] // 2
    values = products([[(weight_rows[pl.ds(n * half, half), :], both)] for n in range(2)])
    value = jnp.concatenate(values, 0)
    value = value[:, :slots] + value[:, slots:]
    partial[...] = value.reshape(count_x, chips, 8, slots)
    copies_out = [
        pltpu.make_async_remote_copy(
            src_ref=partial.at[u, v],
            dst_ref=received.at[u, v],
            send_sem=reduce_send.at[u, v],
            recv_sem=reduce_recv.at[u, v],
            device_id=device(u, 2 * v, 0),
            device_id_type=MESH,
        )
        for u, v in goals
    ]
    for copy in copies_out:
        copy.start()

    for copy in copies_halo:
        copy.wait()

    def prepare(planes, _):
        for part in range(4):
            group = 4 * planes + part
            value = [eight_cells(halo, group, n) for n in range(9)]
            place = [
                jnp.zeros((8, slots), jnp.int32) + 2 * planes + part // 2,
                part % 2 * 2 + cell // 4,
                cell % 4,
            ]
            position = [value[c] + (place[c].astype(f32) - 1.5) for c in range(3)]
            rows, splits = source_values(position, value[3:6], value[6:9])
            store_rows(stage_rows, rows, source_rows, 8 * source_rows * part)
            store_rows(stage_split, splits, split_rows, 8 * split_rows * part)
        for part in range(4):
            group = 4 * planes + part
            pack_sources(
                stage_rows, stage_split, halo_rows, halo_split, group * 8, group * 2, part
            )
        return 0

    lax.fori_loop(0, 2, prepare, 0)
    near_halo()

    def row(refs, n):
        return sum(ref[pl.ds(n, 8, stride=source_rows), :] for ref in refs)

    near_w, near_c = (near_w, halo_w), (near_c, halo_c)

    pairs = [charge[a] * lines[b] for a in range(3) for b in range(3)]
    still = sum(pairs[n] * row(near_w, n) for n in range(9))
    near = []
    for c in range(3):
        first = sum(pairs[n] * row(near_w, 9 + 9 * c + n) for n in range(9))
        second = row(near_c, 36 + c) - sum(position[b] * row(near_c, 3 * b + c) for b in range(3))
        near.append(near_scale * (first - position[c] * still + second))

    stressed = [sum(stress_ref[a, b] * charge[b] for b in range(3)) for a in range(3)]
    applied = crossed(stressed, lines)
    known = [near[c] + applied[c] for c in range(3)]
    shorten = 1.0 / jnp.maximum(sum(lines[c] * lines[c] for c in range(3)), 1.0)
    scale = mobility * mask

    for copy in copies_out:
        copy.wait()
    received[0, 0] = partial[0, 0]
    summed_moments = jnp.sum(received[...].reshape(count_x * chips, 8, slots), 0)
    high, low = high_low(summed_moments)
    left = jnp.concatenate([high, low], 0).astype(bf16)
    left = jnp.concatenate([left, jnp.zeros((16, slots), bf16)], 1)
    groups = []
    for m in range(3):
        right = translation_rows[:, pl.ds(2 * m * slots, 2 * slots)]
        groups.append([(left, jnp.concatenate([right, jnp.zeros((slots, 2 * slots), bf16)], 0))])
    highs, lows = [], []
    for value in products(groups):
        value = value[:8] + value[8:]
        value = value[:, :slots] + value[:, slots:]
        for part, result in zip(high_low(value), (highs, lows)):
            result.append(part + pltpu.roll(part, term_rows, 1))
    left = [jnp.concatenate(parts + [zero], 0).astype(bf16) for parts in (highs, lows)]
    left = jnp.concatenate(left, 1)
    groups = []
    for first in range(0, 8, 2):
        right = jnp.concatenate([poly_rows[first], poly_rows[first + 1]], 1)
        groups.append([(left, jnp.concatenate([right, right], 0))])
    far = [zero] * 3
    for pair, fields in enumerate(products(groups)):
        for m in range(3):
            for n in range(2):
                field = fields[8 * m : 8 * m + 8, n * slots : (n + 1) * slots]
                far[m] = jnp.where(cell == 2 * pair + n, field, far[m])
    far = [value * mask for value in far]

    force = [known[c] + far[c] for c in range(3)]
    along = sum(force[c] * lines[c] for c in range(3))
    along = along * shorten
    for c in range(3):
        out_ref[c] = scale * (force[c] - along * lines[c])


def body(sizes, offsets, lines, burgers, counts, mobility, stress, translation):
    vmem, hbm = (pl.BlockSpec(memory_space=space) for space in (pltpu.VMEM, pltpu.HBM))
    shape = offsets.shape
    flat = (3, 8, slots)
    chips = sizes[1] // 2
    result = pl.pallas_call(
        functools.partial(kernel, sizes),
        out_shape=pltpu.VMEM(flat, f32),
        in_specs=[hbm] * 7,
        out_specs=vmem,
        scratch_shapes=[
            pltpu.VMEM(flat, f32),
            pltpu.VMEM(flat, f32),
            pltpu.VMEM(flat, f32),
            pltpu.SMEM(counts.shape, jnp.int32),
            pltpu.SMEM(mobility.shape, f32),
            pltpu.SMEM(stress.shape, f32),
            pltpu.VMEM(translation.shape, f32),
            pltpu.SemaphoreType.DMA((7,)),
            pltpu.VMEM((4, 4, 4, 16, slots), f32),
            pltpu.VMEM((2, sizes[2], 8, slots), f32),
            pltpu.VMEM((sizes[0], chips, 8, slots), f32),
            pltpu.VMEM((sizes[0], chips, 8, slots), f32),
            pltpu.VMEM((32 * source_rows, slots), f32),
            pltpu.VMEM((32 * split_rows, slots), f32),
            pltpu.VMEM((8 * term_rows, slots), f32),
            pltpu.VMEM((8, 2 * source_rows, 2 * slots), bf16),
            pltpu.VMEM((2, slots, 4 * split_rows), bf16),
            pltpu.VMEM((64, 2 * source_rows, 2 * slots), bf16),
            pltpu.VMEM((16, slots, 4 * split_rows), bf16),
            pltpu.VMEM((8, 4, 4 * split_rows, 2 * slots), bf16),
            pltpu.VMEM((8, slots, slots), bf16),
            pltpu.VMEM((slots, 6 * slots), bf16),
            pltpu.VMEM((sizes[0] * chips * 8, 4 * sizes[2] * 8), bf16),
            pltpu.VMEM((8 * source_rows, slots), f32),
            pltpu.VMEM((8 * source_rows, slots), f32),
            pltpu.VMEM((8 * source_rows, slots), f32),
            pltpu.VMEM((8 * source_rows, slots), f32),
            pltpu.SemaphoreType.DMA((26,)),
            pltpu.SemaphoreType.DMA((26,)),
            pltpu.SemaphoreType.DMA((2, sizes[2])),
            pltpu.SemaphoreType.DMA((2, sizes[2])),
            pltpu.SemaphoreType.DMA((sizes[0], chips)),
            pltpu.SemaphoreType.DMA((sizes[0], chips)),
        ],
        compiler_params=pltpu.CompilerParams(
            collective_id=0, has_side_effects=True, vmem_limit_bytes=60 * 1024 * 1024
        ),
    )(
        offsets.reshape(flat),
        lines.reshape(flat),
        burgers.reshape(flat),
        counts,
        mobility,
        stress,
        translation,
    )
    return result.reshape(shape)


def solution(mesh):
    sizes = tuple(mesh.shape[name] for name in ("gx", "gy", "gz"))
    placed = (
        P(None, "gx", "gy", "gz", None),
        P(None, "gx", "gy", "gz", None),
        P(None, "gx", "gy", "gz", None),
        P("gx", "gy", "gz"),
        P("gx", "gy", "gz"),
        P(),
        P(),
    )
    return jax.shard_map(
        functools.partial(body, sizes),
        mesh=mesh,
        in_specs=placed,
        out_specs=P(None, "gx", "gy", "gz", None),
        check_vma=False,
    )
```
